256 devices in a mesh: inner: 16 (over z, y_hi), outer: 4 (over y_lo, core), head: 4 (over x).
Axes of the slice: x: 4, y: 4 (y_hi: 2, y_lo: 2; y = y_hi * 2 + y_lo), z: 8, core: 2. Of those that a mesh axis runs over, the one named last changes fastest.
Arguments:
- queries: bfloat16 [4, 16384, 128], P('head', ('inner', 'outer')), may hold values from -9 to 9
- key_vectors: bfloat16 [4, 16384, 128], P('head', ('inner', 'outer')), may hold values from -4 to 4
- value_vectors: bfloat16 [4, 16384, 128], P('head', ('inner', 'outer')), may hold values from -5 to 5
- out_grad: bfloat16 [4, 16384, 128], P('head', ('inner', 'outer')), may hold values from -5 to 5
- log_forget: float32 [4, 16384], P('head', ('inner', 'outer')), may hold values from -1.5 to 0
- span_order: int32 [128], replicated, may hold values from 0 to 127, as said below
Outputs:
- query_grad: bfloat16 [4, 16384, 128], P('head', ('inner', 'outer'))
- key_grad: bfloat16 [4, 16384, 128], P('head', ('inner', 'outer'))
- value_grad: bfloat16 [4, 16384, 128], P('head', ('inner', 'outer'))
- forget_grad: float32 [4, 16384], P('head', ('inner', 'outer'))
The draws below stay inside these ranges and needn't reach their ends.
Inputs may be any that keep to these rules, and one draw needn't show every extreme that they name: `span_order`: a permutation of the span numbers; span c covers positions c * 128 to c * 128 + 127; the two slots of one device's rows hold spans whose numbers add up to 127.
All inputs are finite; a program needn't handle non-finite values.
Results may differ from the reference program's by a relative error of at most 0.0075.
Values may be sent and summed in bfloat16 or wider, within the bound.
No kernel may reach another device: no remote copies, remote signals or barrier semaphores. Data moves between devices by JAX's collectives and lax.ppermute only.
A program may use at most 64 MiB of HBM per device.

```python
import math
import jax
import jax.numpy as jnp
from jax import lax

DH = 128
HEAD_TOTAL = 4
SHARDS = 64
SPAN = 128
NCHUNK = 128
SEQUENCE_LENGTH = 16384


def draw_queries(key, part):
    key = jax.random.fold_in(key, 1)
    values = jnp.clip(jax.random.normal(key, (HEAD_TOTAL, SEQUENCE_LENGTH, DH), jnp.float32), -4.0, 4.0)
    return values.astype(jnp.bfloat16)


def draw_key_vectors(key, part):
    key = jax.random.fold_in(key, 2)
    values = jnp.clip(jax.random.normal(key, (HEAD_TOTAL, SEQUENCE_LENGTH, DH), jnp.float32), -4.0, 4.0)
    return values.astype(jnp.bfloat16)


def log_uniform(key, shape, low, high):
    return jnp.exp(jax.random.uniform(key, shape, jnp.float32, math.log(low), math.log(high)))


def draw_log_forget(key, part):
    key = jax.random.fold_in(key, 3)
    order = jax.random.permutation(jax.random.fold_in(key, 11), HEAD_TOTAL)
    keeping = HEAD_TOTAL // 2
    slow_heads = order < keeping
    slow_rate = log_uniform(jax.random.fold_in(key, 12), (HEAD_TOTAL,), 0.1 / SEQUENCE_LENGTH, 0.5 / SEQUENCE_LENGTH)
    fast_rate = log_uniform(jax.random.fold_in(key, 13), (HEAD_TOTAL,), 1.0 / 50.0, 1.0 / 30.0)
    rate = jnp.where(slow_heads, slow_rate, fast_rate)
    block_factor = log_uniform(jax.random.fold_in(key, 14), (HEAD_TOTAL, NCHUNK, 1), 0.6, 1.6)
    rough = jax.random.uniform(jax.random.fold_in(key, 15), (HEAD_TOTAL, NCHUNK, SPAN), jnp.float32, 0.5, 1.5)
    gate_values = -(rate[:, None, None] * block_factor * rough).reshape(HEAD_TOTAL, SEQUENCE_LENGTH)
    group_row_count = jax.random.randint(jax.random.fold_in(key, 16), (HEAD_TOTAL, 2), 0, SEQUENCE_LENGTH)
    group_length = jax.random.uniform(jax.random.fold_in(key, 17), (HEAD_TOTAL, 2), jnp.float32, 0.22, 0.69)
    match_count = (jnp.arange(SEQUENCE_LENGTH)[None, None, :] == group_row_count[:, :, None]).astype(jnp.float32)
    gate_values = gate_values - jnp.sum(match_count * group_length[:, :, None], axis=1)
    return gate_values.astype(jnp.float32)


def draw_span_order(key, part):
    key = jax.random.fold_in(key, 4)
    placing = jax.random.permutation(key, SHARDS)
    paired = jnp.stack([placing, NCHUNK - 1 - placing], axis=1)
    return paired.reshape(NCHUNK).astype(jnp.int32)


def block_levels(stream_key, shape, split, smallest, top_value):
    level, own = 1.0, jax.random.fold_in(stream_key, 6)
    for axis_at, blocks in split:
        steps = jnp.exp(jax.random.uniform(jax.random.fold_in(own, axis_at), (blocks,), jnp.float32, smallest / len(split), top_value / len(split)))
        level = level * jnp.repeat(steps, shape[axis_at] // blocks).reshape([-1 if axis == axis_at else 1 for axis in range(len(shape))])
    return level


def noise(own_key, dims, width, limit, pieces=(), kind=jnp.bfloat16):
    drawn = width * jax.random.normal(own_key, dims, jnp.float32)
    if pieces:
        drawn = drawn * block_levels(own_key, dims, pieces, -0.22, 0.18)
    return jnp.clip(drawn, -limit, limit).astype(kind)


def setup_inputs(seed: int = 0) -> dict:
    arg_keys = jax.random.split(jax.random.key(seed), 7)
    return {
        "queries": draw_queries(jax.random.fold_in(arg_keys[6], 71), 0),
        "key_vectors": draw_key_vectors(jax.random.fold_in(arg_keys[6], 71), 0),
        "value_vectors": noise(arg_keys[2], (HEAD_TOTAL, SEQUENCE_LENGTH, DH), 1.0, 5.0, ((0, 4), (1, 64))),
        "out_grad": noise(arg_keys[3], (HEAD_TOTAL, SEQUENCE_LENGTH, DH), 1.0, 5.0, ((0, 4), (1, 64))),
        "log_forget": draw_log_forget(jax.random.fold_in(arg_keys[6], 71), 0),
        "span_order": draw_span_order(jax.random.fold_in(arg_keys[6], 71), 0),
    }


def reference(queries, key_vectors, value_vectors, out_grad, log_forget, span_order):
    offsets = jnp.arange(SPAN, dtype=jnp.int32)
    positions = (span_order[:, None].astype(jnp.int32) * SPAN + offsets[None, :]).reshape(SEQUENCE_LENGTH)
    ordered = jnp.zeros_like(log_forget).at[:, positions].set(log_forget)
    prefix = jnp.cumsum(ordered, axis=1)[:, positions]
    score_scale = 1.0 / math.sqrt(DH)
    block_size = min(512, SEQUENCE_LENGTH)
    block_count = SEQUENCE_LENGTH // block_size
    query_list = []
    key_list = []
    value_list = []
    forget_list = []
    for head_index in range(HEAD_TOTAL):
        query_all = queries[head_index]
        key_all = key_vectors[head_index]
        value_all = value_vectors[head_index]
        grad_all = out_grad[head_index]
        prefix_all = prefix[head_index]

        def single_block(carry, block_index):
            key_acc, value_acc, prefix_acc = carry
            first = (block_index * block_size).astype(jnp.int32)
            query_matrix = lax.dynamic_slice_in_dim(query_all, first, block_size, 0)
            grad_rows = lax.dynamic_slice_in_dim(grad_all, first, block_size, 0)
            row_prefix = lax.dynamic_slice_in_dim(prefix_all, first, block_size, 0)
            row_pos = lax.dynamic_slice_in_dim(positions, first, block_size, 0)
            scores = jnp.dot(query_matrix, key_all.T, preferred_element_type=jnp.float32) * score_scale
            scores = scores + row_prefix[:, None] - prefix_all[None, :]
            allowed = positions[None, :] <= row_pos[:, None]
            best = lax.optimization_barrier(jnp.max(jnp.where(allowed, scores, -1e+30), axis=1))
            total = lax.optimization_barrier(jnp.sum(jnp.where(allowed, jnp.exp(scores - best[:, None]), 0.0), axis=1))
            row_lse = best + jnp.log(total)
            weights = jnp.where(allowed, jnp.exp(scores - row_lse[:, None]), 0.0)
            upstream = jnp.dot(grad_rows, value_all.T, preferred_element_type=jnp.float32)
            delta = lax.optimization_barrier(jnp.sum(weights * upstream, axis=1))
            score_grad = weights * (upstream - delta[:, None])
            score_low = score_grad.astype(jnp.bfloat16)
            weights_low = weights.astype(jnp.bfloat16)
            query_block = (score_scale * jnp.dot(score_low, key_all, preferred_element_type=jnp.float32)).astype(jnp.bfloat16)
            key_acc = key_acc + score_scale * jnp.dot(score_low.T, query_matrix, preferred_element_type=jnp.float32)
            value_acc = value_acc + jnp.dot(weights_low.T, grad_rows, preferred_element_type=jnp.float32)
            prefix_acc = prefix_acc - lax.optimization_barrier(jnp.sum(score_grad, axis=0))
            return ((key_acc, value_acc, prefix_acc), query_block)
        start_carry = (jnp.zeros((SEQUENCE_LENGTH, DH), jnp.float32), jnp.zeros((SEQUENCE_LENGTH, DH), jnp.float32), jnp.zeros((SEQUENCE_LENGTH,), jnp.float32))
        closing_carry, query_blocks = lax.scan(single_block, start_carry, jnp.arange(block_count, dtype=jnp.int32))
        key_acc, value_acc, prefix_acc = closing_carry
        query_list.append(query_blocks.reshape(SEQUENCE_LENGTH, DH))
        key_list.append(key_acc.astype(jnp.bfloat16))
        value_list.append(value_acc.astype(jnp.bfloat16))
        placed = jnp.zeros((SEQUENCE_LENGTH,), jnp.float32).at[positions].set(prefix_acc)
        suffix = jnp.flip(jnp.cumsum(jnp.flip(placed)))
        forget_list.append(suffix[positions])
    return (jnp.stack(query_list), jnp.stack(key_list), jnp.stack(value_list), jnp.stack(forget_list))
```

```python
import math

import jax
import jax.numpy as jnp
from jax import lax
from jax.experimental import pallas as pl
from jax.experimental.pallas import tpu as pltpu
from jax.sharding import Mesh, PartitionSpec as P

F32 = jnp.float32
BF16 = jnp.bfloat16
LOG2E = 1.4426950408889634
NEG = -1e30
GROUP = 8
HALF = 128
ROWS = 256
AUX = 16
PACK = ROWS + AUX
NEAR = (0, 1, -1, 2, -2, 3, -3, 4)
Z, Y, C = "z", ("y_hi", "y_lo"), "core"
COLUMN = ("y_hi", "y_lo", "core")
VMEM_LIMIT = 48 * 1024 * 1024
vmem = pl.BlockSpec(memory_space=pltpu.VMEM)
smem = pl.BlockSpec(memory_space=pltpu.SMEM)
hbm = pl.BlockSpec(memory_space=pl.ANY)


def call(kernel, outs, in_specs, scratch=(), flops=0):
    return pl.pallas_call(
        kernel,
        out_shape=outs,
        in_specs=in_specs,
        out_specs=jax.tree.map(lambda _: vmem, outs),
        scratch_shapes=list(scratch),
        compiler_params=pltpu.CompilerParams(vmem_limit_bytes=VMEM_LIMIT),
        cost_estimate=pl.CostEstimate(flops=flops, bytes_accessed=4 << 20, transcendentals=0),
    )


def dot(a, b, ca, cb):
    return lax.dot_general(a, b, (((ca,), (cb,)), ((), ())), preferred_element_type=F32)


def split_rows(row, first=0):
    high = row.astype(BF16).astype(F32)
    middle = (row - high).astype(BF16).astype(F32)
    low = row - high - middle
    at = lax.broadcasted_iota(jnp.int32, (AUX, row.shape[1]), 0) - first
    return jnp.where(at == 0, high, jnp.where(at == 1, middle, jnp.where(at == 2, low, 0.0)))


def join_rows(rows, first=0):
    rows = rows.astype(F32)
    return rows[first : first + 1] + rows[first + 1 : first + 2] + rows[first + 2 : first + 3]


def running_sum(row):
    lane = lax.broadcasted_iota(jnp.int32, row.shape, 1)
    step = 1
    while step < HALF:
        row = row + jnp.where(lane >= step, pltpu.roll(row, step, 1), 0.0)
        step *= 2
    return row


def pack_kernel(swap_ref, q_ref, k_ref, v_ref, g_ref, f_ref, qg_ref, kv_ref):
    swap = swap_ref[0]
    for half in range(2):
        source = pl.ds(pl.multiple_of(HALF * (half ^ swap), HALF), HALF)
        target = pl.ds(HALF * half, HALF)
        qg_ref[target, 0:HALF] = q_ref[source, :]
        qg_ref[target, HALF:ROWS] = g_ref[source, :]
        kv_ref[target, 0:HALF] = k_ref[source, :]
        kv_ref[target, HALF:ROWS] = v_ref[source, :]
    gates = [f_ref[0:1, 0:HALF], f_ref[0:1, HALF:ROWS]]
    for half in range(2):
        gate = jnp.where(swap == 1, gates[1 - half], gates[half])
        rows = split_rows(running_sum(gate)).astype(BF16)
        qg_ref[ROWS:PACK, HALF * half : HALF * (half + 1)] = rows
        kv_ref[ROWS:PACK, HALF * half : HALF * (half + 1)] = rows


def totals_kernel(*refs):
    blocks, out_ref, aux, sems = refs[:8], refs[8], refs[9], refs[10]
    copies = []
    for at, block in enumerate(blocks):
        last = block.shape[0] - AUX
        copies.append(pltpu.make_async_copy(block.at[pl.ds(last, AUX), :], aux.at[at], sems.at[at]))
    for copy in copies:
        copy.start()
    lane = lax.broadcasted_iota(jnp.int32, (1, HALF), 1)
    total = jnp.zeros((1, HALF), F32)
    for at, copy in enumerate(copies):
        copy.wait()
        row = join_rows(aux[at])
        for half in range(2):
            value = row[:, HALF * (half + 1) - 1 : HALF * (half + 1)]
            total = jnp.where(lane == 2 * at + half, value, total)
    out_ref[...] = total


def load_blocks(index_ref, query_refs, key_refs, qs, ks, sems):
    copies = []

    def add(source, target):
        copies.append(pltpu.make_async_copy(source, target, sems.at[len(copies)]))

    for at, ref in enumerate(query_refs):
        add(ref, qs.at[index_ref[16 + at]])
    for at, ref in enumerate(key_refs[:7]):
        add(ref, ks.at[at])
    add(key_refs[7], ks.at[7, pl.ds(HALF, HALF + AUX), :])
    add(key_refs[8], ks.at[7, pl.ds(0, HALF), :])
    for copy in copies:
        copy.start()
    for copy in copies:
        copy.wait()


def span_gates(qs, wq):
    for d in range(GROUP):
        row = join_rows(qs[d, ROWS:PACK, :]) * LOG2E
        wq[0, d : d + 1, :] = row[:, 0:HALF]
        wq[1, d : d + 1, :] = row[:, HALF:ROWS]


def gate_columns(ks, e, columns):
    row = join_rows(ks[e, ROWS:PACK, :]) * LOG2E
    for half in range(2):
        part = row[:, HALF * half : HALF * (half + 1)]
        columns[half] = jnp.transpose(jnp.broadcast_to(part, (HALF, HALF)))


def half_rows(half):
    return pl.ds(pl.multiple_of(HALF * half, HALF), HALF)


def stats_kernel(scale, index_ref, *refs):
    query_refs, key_refs = refs[:8], refs[8:17]
    one_ref, two_ref, own_ref = refs[17:20]
    qs, ks, wq, columns, sems = refs[20:]
    load_blocks(index_ref, query_refs, key_refs, qs, ks, sems)
    span_gates(qs, wq)
    own = index_ref[24]
    ahead = lax.broadcasted_iota(jnp.int32, (HALF, HALF), 0) - lax.broadcasted_iota(
        jnp.int32, (HALF, HALF), 1
    )

    def tile_stats(scores, upstream):
        best = jnp.max(scores, axis=0, keepdims=True)
        factor = jnp.exp2(scores - best)
        return (
            best,
            jnp.sum(factor, axis=0, keepdims=True),
            jnp.sum(factor * upstream, axis=0, keepdims=True),
        )

    def key_block(e, carry):
        gate_columns(ks, e, columns)
        key_low, value_low = ks[e, 0:HALF, 0:HALF], ks[e, 0:HALF, HALF:ROWS]
        column = columns[0]
        for pair in range(GROUP // 2):
            q = jnp.concatenate([qs[2 * pair + i, HALF:ROWS, 0:HALF] for i in range(2)], 0)
            g = jnp.concatenate([qs[2 * pair + i, HALF:ROWS, HALF:ROWS] for i in range(2)], 0)
            w = jnp.concatenate([wq[1, 2 * pair + i : 2 * pair + i + 1, :] for i in range(2)], 1)
            column2 = jnp.concatenate([column, column], 1)
            scores = dot(key_low, q, 1, 1) * scale + (w - column2)
            upstream = dot(value_low, g, 1, 1)
            for at, row in enumerate(tile_stats(scores, upstream)):
                one_ref[e, at : at + 1, pl.ds(2 * HALF * pair, 2 * HALF)] = row
        for d in range(GROUP):
            half = (index_ref[8 + e] > index_ref[d]).astype(jnp.int32)
            rows = half_rows(half)
            limit = jnp.where((e == 0) & (own == d), 0, HALF)
            scores = dot(ks[e, rows, 0:HALF], qs[d, rows, 0:HALF], 1, 1) * scale + (
                wq[half, d : d + 1, :] - columns[half]
            )
            scores = jnp.where(ahead <= limit, scores, NEG)
            upstream = dot(ks[e, rows, HALF:ROWS], qs[d, rows, HALF:ROWS], 1, 1)
            for at, row in enumerate(tile_stats(scores, upstream)):
                two_ref[e, at : at + 1, pl.ds(HALF * d, HALF)] = row
        return carry

    lax.fori_loop(0, GROUP, key_block, 0)
    gate_columns(ks, 0, columns)
    w = wq[1, pl.ds(own, 1), :]
    scores = dot(ks[0, HALF:ROWS, 0:HALF], qs[own, HALF:ROWS, 0:HALF], 1, 1) * scale + (
        w - columns[1]
    )
    scores = jnp.where(ahead <= 0, scores, NEG)
    upstream = dot(ks[0, HALF:ROWS, HALF:ROWS], qs[own, HALF:ROWS, HALF:ROWS], 1, 1)
    for at, row in enumerate(tile_stats(scores, upstream)):
        own_ref[at : at + 1, :] = row


def merge_kernel(
    index_ref, spans_ref, ids_ref, t0, t1, t2, t3, one_ref, two_ref, own_ref, out_ref, place_ref
):
    own = index_ref[24]
    ids = ids_ref[...]
    totals = jnp.concatenate([t0[...], t1[...], t2[...], t3[...]], 0)
    places = []
    for at in range(4 * GROUP):
        before = jnp.where((ids >= 0) & (ids < spans_ref[at]), totals, 0.0)
        place = jnp.sum(jnp.sum(before, axis=0, keepdims=True), axis=1, keepdims=True) * LOG2E
        places.append(jnp.broadcast_to(place, (1, HALF)))
        place_ref[at : at + 1, :] = places[-1]
    key_low = jnp.concatenate(places[0:8], 0)
    key_high = jnp.concatenate(places[8:16], 0)
    sub = lax.broadcasted_iota(jnp.int32, (GROUP, HALF), 0)
    key_rank = jnp.zeros((GROUP, HALF), jnp.int32)
    for e in range(GROUP):
        key_rank = jnp.where(sub == e, index_ref[8 + e], key_rank)

    def finish(best, total, weighted, at, d):
        some = total > 0.0
        safe = jnp.where(some, total, 1.0)
        lse = jnp.where(some, best + jnp.log2(safe), NEG)
        delta = jnp.where(some, weighted / safe, 0.0)
        for copy in range(GROUP):
            out_ref[copy, at + d : at + d + 1, :] = lse
            out_ref[copy, at + 8 + d : at + 9 + d, :] = delta

    def down(x):
        return jnp.sum(x, axis=0, keepdims=True)

    for d in range(GROUP):
        lanes = slice(HALF * d, HALF * (d + 1))
        high = key_rank > index_ref[d]
        query_low, query_high = places[16 + d], places[24 + d]
        first = one_ref[:, 0, lanes] + (query_high - key_low)
        second = two_ref[:, 0, lanes] + jnp.where(high, query_high - key_high, query_low - key_low)
        mine = own == d
        third = jnp.where(mine, own_ref[0:1, :], NEG)
        best = jnp.maximum(
            jnp.max(jnp.maximum(first, jnp.where(high, second, NEG)), axis=0, keepdims=True), third
        )
        first_weight = jnp.exp2(first - best)
        second_weight = jnp.where(high, jnp.exp2(second - best), 0.0)
        third_weight = jnp.where(mine, jnp.exp2(third - best), 0.0)
        sums = [
            down(one_ref[:, at, lanes] * first_weight + two_ref[:, at, lanes] * second_weight)
            + own_ref[at : at + 1, :] * third_weight
            for at in (1, 2)
        ]
        finish(best, sums[0], sums[1], 0, d)
        low = jnp.where(high, NEG, second)
        best = jnp.max(low, axis=0, keepdims=True)
        weight = jnp.where(high, 0.0, jnp.exp2(low - best))
        sums = [down(two_ref[:, at, lanes] * weight) for at in (1, 2)]
        finish(best, sums[0], sums[1], 16, d)


def grads_kernel(scale, index_ref, stats_ref, place_ref, *refs):
    query_refs, key_refs = refs[:8], refs[8:17]
    dq_ref, dkv_ref, aux_ref = refs[17:20]
    qs, ks, wq, columns, delta, dqt, dk, dv, pg, totals, sems = refs[20:]
    load_blocks(index_ref, query_refs, key_refs, qs, ks, sems)
    span_gates(qs, wq)
    own = index_ref[24]
    ahead = lax.broadcasted_iota(jnp.int32, (HALF, HALF), 0) - lax.broadcasted_iota(
        jnp.int32, (HALF, HALF), 1
    )
    for half, at in ((1, 0), (0, 16)):
        lse = [stats_ref[b, at : at + 8, :] for b in range(GROUP)]
        best = lse[0]
        for b in range(1, GROUP):
            best = jnp.maximum(best, lse[b])
        total = jnp.zeros((GROUP, HALF), F32)
        weighted = jnp.zeros((GROUP, HALF), F32)
        for b in range(GROUP):
            weight = jnp.exp2(lse[b] - best)
            total = total + weight
            weighted = weighted + weight * stats_ref[b, at + 8 : at + 16, :]
        wq[half] = wq[half] - (best + jnp.log2(total))
        delta[half] = weighted / total
    dqt[...] = jnp.zeros_like(dqt)
    totals[...] = jnp.zeros_like(totals)
    lane = lax.broadcasted_iota(jnp.int32, (1, HALF), 1)
    inverse = 1.0 / math.sqrt(HALF)

    def query_gate(half, d, key_place):
        place = place_ref[pl.ds(16 + 8 * half + d, 1), :]
        return wq[half, d : d + 1, :] + (place - key_place)

    def key_block(e, carry):
        gate_columns(ks, e, columns)
        dk[...] = jnp.zeros_like(dk)
        dv[...] = jnp.zeros_like(dv)
        pg[...] = jnp.zeros_like(pg)
        key_low, value_low = ks[e, 0:HALF, 0:HALF], ks[e, 0:HALF, HALF:ROWS]
        turned = jnp.transpose(key_low)
        column = columns[0]
        column2 = jnp.concatenate([column, column], 1)
        place = place_ref[pl.ds(e, 1), :]
        for pair in range(GROUP // 2):
            both = (2 * pair, 2 * pair + 1)
            q = jnp.concatenate([qs[d, HALF:ROWS, 0:HALF] for d in both], 0)
            g = jnp.concatenate([qs[d, HALF:ROWS, HALF:ROWS] for d in both], 0)
            w = jnp.concatenate([query_gate(1, d, place) for d in both], 1)
            shift = jnp.concatenate([delta[1, d : d + 1, :] for d in both], 1)
            probs = jnp.exp2(dot(key_low, q, 1, 1) * scale + (w - column2))
            grads = probs * (dot(value_low, g, 1, 1) - shift)
            low_grads = grads.astype(BF16)
            dv[0] += dot(probs.astype(BF16), g, 1, 0)
            dk[0] += dot(low_grads, q, 1, 0)
            part = dot(turned, low_grads, 1, 0)
            dqt[1, both[0]] += part[:, 0:HALF]
            dqt[1, both[1]] += part[:, HALF:ROWS]
            pg[0] += grads[:, 0:HALF] + grads[:, HALF:ROWS]

        def tile(rows, half, d, limit):
            k, v = ks[e, rows, 0:HALF], ks[e, rows, HALF:ROWS]
            q, g = qs[d, rows, 0:HALF], qs[d, rows, HALF:ROWS]
            w = query_gate(half, d, place_ref[pl.ds(8 * half + e, 1), :])
            scores = dot(k, q, 1, 1) * scale + (w - columns[half])
            probs = jnp.where(ahead <= limit, jnp.exp2(scores), 0.0)
            grads = probs * (dot(v, g, 1, 1) - delta[half, pl.ds(d, 1), :])
            low_grads = grads.astype(BF16)
            dv[half] += dot(probs.astype(BF16), g, 1, 0)
            dk[half] += dot(low_grads, q, 1, 0)
            dqt[half, d] += dot(k, low_grads, 0, 0)
            pg[half] += grads

        for d in range(GROUP):
            half = (index_ref[8 + e] > index_ref[d]).astype(jnp.int32)
            tile(half_rows(half), half, d, jnp.where((e == 0) & (own == d), 0, HALF))

        @pl.when(e == 0)
        def _():
            k, v = ks[e, HALF:ROWS, 0:HALF], ks[e, HALF:ROWS, HALF:ROWS]
            q, g = qs[own, HALF:ROWS, 0:HALF], qs[own, HALF:ROWS, HALF:ROWS]
            scores = dot(k, q, 1, 1) * scale + (wq[1, pl.ds(own, 1), :] - columns[1])
            probs = jnp.where(ahead <= 0, jnp.exp2(scores), 0.0)
            grads = probs * (dot(v, g, 1, 1) - delta[1, pl.ds(own, 1), :])
            low_grads = grads.astype(BF16)
            dv[1] += dot(probs.astype(BF16), g, 1, 0)
            dk[1] += dot(low_grads, q, 1, 0)
            dqt[1, own] += dot(k, low_grads, 0, 0)
            pg[1] += grads

        slot = index_ref[25 + e]
        for half in range(2):
            rows = slice(HALF * half, HALF * (half + 1))
            dkv_ref[slot, rows, 0:HALF] = (dk[half] * inverse).astype(BF16)
            dkv_ref[slot, rows, HALF:ROWS] = dv[half].astype(BF16)
            row = -jnp.sum(jnp.transpose(pg[half]), axis=0, keepdims=True)
            aux_ref[slot, :, rows] = split_rows(row)
            total = jnp.sum(row, axis=1, keepdims=True)
            totals[...] = jnp.where(lane == 2 * e + half, total, totals[...])
        return carry

    lax.fori_loop(0, GROUP, key_block, 0)
    rows = split_rows(totals[...]).astype(BF16)
    for d in range(GROUP):
        for half in range(2):
            part = jnp.transpose(dqt[half, d]) * inverse
            dq_ref[d, HALF * half : HALF * (half + 1), :] = part.astype(BF16)
        dq_ref[d, ROWS:PACK, :] = rows


def query_kernel(index_ref, spans_ref, ids_ref, parts_ref, aux_ref, dq_ref, out_ref):
    swap = index_ref[33]
    for half in range(2):
        rows = slice(HALF * half, HALF * (half + 1))
        total = parts_ref[0, rows, :].astype(F32)
        for b in range(1, GROUP):
            total = total + parts_ref[b, rows, :].astype(F32)
        dq_ref[half_rows(half ^ swap), :] = total.astype(BF16)
    totals = jnp.concatenate([join_rows(parts_ref[b, ROWS:PACK, :]) for b in range(GROUP)], 0)
    ids = ids_ref[...]
    for e in range(GROUP):
        slot = index_ref[25 + e]
        for half in range(2):
            lanes = slice(HALF * half, HALF * (half + 1))
            beyond = jnp.where(ids > spans_ref[8 * half + e], totals, 0.0)
            value = jnp.sum(jnp.sum(beyond, axis=0, keepdims=True), axis=1, keepdims=True)
            row = jnp.broadcast_to(value, (1, HALF))
            out_ref[slot, :, lanes] = (aux_ref[slot, :, lanes] + split_rows(row, 3)).astype(BF16)


def key_kernel(index_ref, parts_ref, dk_ref, dv_ref, f_ref):
    swap = index_ref[33]
    for half in range(2):
        rows = slice(HALF * half, HALF * (half + 1))
        total = parts_ref[0, rows, :].astype(F32)
        for z in range(1, GROUP):
            total = total + parts_ref[z, rows, :].astype(F32)
        total = total.astype(BF16)
        dk_ref[half_rows(half ^ swap), :] = total[:, 0:HALF]
        dv_ref[half_rows(half ^ swap), :] = total[:, HALF:ROWS]
    aux = parts_ref[0, ROWS:PACK, :].astype(F32)
    for z in range(1, GROUP):
        aux = aux + parts_ref[z, ROWS:PACK, :].astype(F32)
    halves = []
    for half in range(2):
        lanes = slice(HALF * half, HALF * (half + 1))
        row = join_rows(aux[:, lanes])
        total = jnp.sum(row, axis=1, keepdims=True)
        halves.append(total - running_sum(row) + row + join_rows(aux[:, lanes], 3))
    for half in range(2):
        lanes = slice(HALF * half, HALF * (half + 1))
        f_ref[:, lanes] = jnp.where(swap == 1, halves[1 - half], halves[half])


def fetch(x, axis, size, offset):
    return lax.ppermute(x, axis, [((i + offset) % size, i) for i in range(size)])


def local(queries, key_vectors, value_vectors, out_grad, log_forget, span_order):
    scale = LOG2E / math.sqrt(HALF)
    z, y, core = lax.axis_index(Z), lax.axis_index(Y), lax.axis_index(C)
    column = y * 2 + core
    pairs = span_order.reshape(64, 2)
    lows, highs = jnp.min(pairs, axis=1), jnp.max(pairs, axis=1)
    swaps = (pairs[:, 0] > pairs[:, 1]).astype(jnp.int32)
    device = jnp.arange(64, dtype=jnp.int32)

    def pick(table, which):
        match = which[..., None] == device
        return jnp.sum(jnp.where(match, table, 0), axis=-1)

    near = jnp.array(NEAR, jnp.int32)
    z_slots = (z + near) % GROUP
    y_order = (y + jnp.array([0, 1, -1, 2], jnp.int32)) % 4
    core_order = jnp.stack([core, 1 - core])
    columns = y_order[:, None] * 2 + core_order[None, :]
    every = jnp.arange(GROUP, dtype=jnp.int32)
    query_devices, key_devices = z * GROUP + every, z_slots * GROUP + column
    swap = pick(swaps, z * GROUP + column)[None]
    index = jnp.concatenate(
        [
            pick(lows, query_devices),
            pick(lows, key_devices),
            columns.T.reshape(GROUP),
            column[None],
            z_slots,
            swap,
        ]
    ).astype(jnp.int32)
    spans = jnp.concatenate(
        [pick(t, which) for which in (key_devices, query_devices) for t in (lows, highs)]
    )

    def span_ids(order):
        which = z_slots[None, :] * GROUP + order[:, None]
        ids = jnp.stack([pick(lows, which), pick(highs, which)], axis=2).reshape(GROUP, 16)
        return jnp.pad(ids, ((0, 0), (0, HALF - 16)), constant_values=-1)

    near_ids, every_ids = span_ids(columns.reshape(GROUP)), span_ids(every)

    packed = jax.ShapeDtypeStruct((PACK, ROWS), BF16)
    qg, kv = call(pack_kernel, (packed, packed), [smem] + [vmem] * 5)(
        swap, queries[0], key_vectors[0], value_vectors[0], out_grad[0], log_forget
    )
    up1, down1, up2, down2 = [fetch(kv, Z, 8, o) for o in (1, -1, 2, -2)]
    mine = [qg] + [fetch(qg, Y, 4, o) for o in (1, -1, 2)]
    up3, down3 = fetch(up2, Z, 8, 1), fetch(down2, Z, 8, -1)
    across = [fetch(block, C, 2, 1) for block in mine]
    far_low = fetch(down2[:HALF], Z, 8, -2)
    far_high = fetch(up2[HALF:], Z, 8, 2)
    query_blocks = mine + across
    key_blocks = [kv, up1, down1, up2, down2, up3, down3, far_high, far_low]

    total = call(
        totals_kernel,
        jax.ShapeDtypeStruct((1, HALF), F32),
        [hbm] * 8,
        [pltpu.VMEM((8, AUX, ROWS), BF16), pltpu.SemaphoreType.DMA((8,))],
    )(*key_blocks[:8])
    chip_totals = jnp.concatenate([total, fetch(total, C, 2, 1)], 0)
    totals = [chip_totals] + [fetch(chip_totals, Y, 4, o) for o in (1, -1, 2)]

    blocks = [
        pltpu.VMEM((GROUP, PACK, ROWS), BF16),
        pltpu.VMEM((GROUP, PACK, ROWS), BF16),
        pltpu.VMEM((2, GROUP, HALF), F32),
        pltpu.VMEM((2, HALF, HALF), F32),
    ]
    sems = pltpu.SemaphoreType.DMA((17,))
    tiles = jax.ShapeDtypeStruct((GROUP, 3, GROUP * HALF), F32)
    one, two, own = call(
        lambda *refs: stats_kernel(scale, *refs),
        (tiles, tiles, jax.ShapeDtypeStruct((GROUP, HALF), F32)),
        [smem] + [hbm] * 17,
        blocks + [sems],
        flops=1 << 31,
    )(index, *query_blocks, *key_blocks)
    stats, place = call(
        merge_kernel,
        (
            jax.ShapeDtypeStruct((GROUP, 32, HALF), F32),
            jax.ShapeDtypeStruct((32, HALF), F32),
        ),
        [smem, smem] + [vmem] * 8,
    )(index, spans, near_ids, *totals, one, two, own)
    stats = lax.all_to_all(stats, COLUMN, 0, 0, tiled=True)
    dq_parts, dkv_parts, aux = call(
        lambda *refs: grads_kernel(scale, *refs),
        (
            jax.ShapeDtypeStruct((GROUP, PACK, HALF), BF16),
            jax.ShapeDtypeStruct((GROUP, PACK, ROWS), BF16),
            jax.ShapeDtypeStruct((GROUP, AUX, ROWS), F32),
        ),
        [smem, vmem, vmem] + [hbm] * 17,
        blocks
        + [
            pltpu.VMEM((2, GROUP, HALF), F32),
            pltpu.VMEM((2, GROUP, HALF, HALF), F32),
            pltpu.VMEM((2, HALF, HALF), F32),
            pltpu.VMEM((2, HALF, HALF), F32),
            pltpu.VMEM((2, HALF, HALF), F32),
            pltpu.VMEM((1, HALF), F32),
            sems,
        ],
        flops=1 << 32,
    )(index, stats, place, *query_blocks, *key_blocks)
    dq_parts = lax.all_to_all(dq_parts, COLUMN, 0, 0, tiled=True)
    dq, aux = call(
        query_kernel,
        (
            jax.ShapeDtypeStruct((ROWS, HALF), BF16),
            jax.ShapeDtypeStruct((GROUP, AUX, ROWS), BF16),
        ),
        [smem, smem] + [vmem] * 3,
    )(index, spans, every_ids, dq_parts, aux)
    dkv_parts = lax.dynamic_update_slice(dkv_parts, aux, (0, ROWS, 0))
    dkv_parts = lax.all_to_all(dkv_parts, Z, 0, 0, tiled=True)
    rows = jax.ShapeDtypeStruct((ROWS, HALF), BF16)
    dk, dv, forget = call(
        key_kernel, (rows, rows, jax.ShapeDtypeStruct((1, ROWS), F32)), [smem, vmem]
    )(index, dkv_parts)
    return dq[None], dk[None], dv[None], forget


def solution(mesh):
    fine = Mesh(mesh.devices.reshape(8, 2, 2, 2, 4), ("z", "y_hi", "y_lo", "core", "head"))
    rows = ("z", "y_hi", "y_lo", "core")
    wide, thin = P("head", rows, None), P("head", rows)
    return jax.shard_map(
        local,
        mesh=fine,
        in_specs=(wide, wide, wide, wide, thin, P()),
        out_specs=(wide, wide, wide, thin),
        check_vma=False,
    )
```

```python
import math

import jax
import jax.numpy as jnp
from jax import lax
from jax.experimental import pallas as pl
from jax.experimental.pallas import tpu as pltpu
from jax.sharding import Mesh, PartitionSpec as P

F32 = jnp.float32
BF16 = jnp.bfloat16
LOG2E = 1.4426950408889634
NEG = -1e30
GROUP = 8
HALF = 128
ROWS = 256
AUX = 16
PACK = ROWS + AUX
NEAR = (0, 1, -1, 2, -2, 3, -3, 4)
Z, Y, C = "z", ("y_hi", "y_lo"), "core"
COLUMN = ("y_hi", "y_lo", "core")
VMEM_LIMIT = 20 * 1024 * 1024
vmem = pl.BlockSpec(memory_space=pltpu.VMEM)
smem = pl.BlockSpec(memory_space=pltpu.SMEM)
hbm = pl.BlockSpec(memory_space=pl.ANY)


def call(kernel, outs, in_specs, scratch=(), flops=0, out_spec=None, limit=VMEM_LIMIT):
    return pl.pallas_call(
        kernel,
        out_shape=outs,
        in_specs=in_specs,
        out_specs=out_spec or jax.tree.map(lambda _: vmem, outs),
        scratch_shapes=list(scratch),
        compiler_params=pltpu.CompilerParams(vmem_limit_bytes=limit),
        cost_estimate=pl.CostEstimate(flops=flops, bytes_accessed=4 << 20, transcendentals=0),
    )


def dot(a, b, ca, cb):
    return lax.dot_general(a, b, (((ca,), (cb,)), ((), ())), preferred_element_type=F32)


def split_rows(row, first=0):
    high = row.astype(BF16).astype(F32)
    middle = (row - high).astype(BF16).astype(F32)
    low = row - high - middle
    at = lax.broadcasted_iota(jnp.int32, (AUX, row.shape[1]), 0) - first
    return jnp.where(at == 0, high, jnp.where(at == 1, middle, jnp.where(at == 2, low, 0.0)))


def join_rows(rows, first=0):
    rows = rows.astype(F32)
    return rows[first : first + 1] + rows[first + 1 : first + 2] + rows[first + 2 : first + 3]


def running_sum(row):
    lane = lax.broadcasted_iota(jnp.int32, row.shape, 1)
    step = 1
    while step < HALF:
        row = row + jnp.where(lane >= step, pltpu.roll(row, step, 1), 0.0)
        step *= 2
    return row


def place_of():
    z, y, core = lax.axis_index(Z), lax.axis_index("y_hi") * 2 + lax.axis_index("y_lo"), lax.axis_index(C)
    return z, y, core, y * 2 + core


def slot_low(span_ref, slot):
    return jnp.minimum(span_ref[2 * slot], span_ref[2 * slot + 1])


def own_swap(span_ref):
    z, _, _, column = place_of()
    slot = 2 * (z * GROUP + column)
    return (span_ref[slot] > span_ref[slot + 1]).astype(jnp.int32)


def near_z(z, e):
    return lax.rem(z + (NEAR[e] + GROUP), GROUP)


def near_column(y, core, at):
    offset, other = (0, 1, 3, 2)[at // 2], at % 2
    return lax.rem(y + offset, 4) * 2 + (1 - core if other else core)


def half_rows(half):
    return pl.ds(pl.multiple_of(HALF * half, HALF), HALF)


def table_lanes(table, z, own, low, high):
    sub = lax.broadcasted_iota(jnp.int32, (GROUP, HALF), 0)
    lane = lax.broadcasted_iota(jnp.int32, (GROUP, HALF), 1)
    table = jnp.where((sub == z) & (lane == 2 * own), low, table)
    return jnp.where((sub == z) & (lane == 2 * own + 1), high, table)


def pack_kernel(
    span_ref, q_ref, k_ref, v_ref, g_ref, f_ref, qg_ref, kv_ref, qg, kv, sems
):
    swap = own_swap(span_ref)
    copies = []
    for half in range(2):
        source = half_rows(jnp.bitwise_xor(half, swap))
        target = pl.ds(HALF * half, HALF)
        for ref, out, lanes in (
            (k_ref, kv, pl.ds(0, HALF)),
            (v_ref, kv, pl.ds(HALF, HALF)),
            (q_ref, qg, pl.ds(0, HALF)),
            (g_ref, qg, pl.ds(HALF, HALF)),
        ):
            copies.append((ref.at[source, :], out.at[target, lanes]))
    copies = [pltpu.make_async_copy(a, b, sems.at[i]) for i, (a, b) in enumerate(copies)]
    for copy in copies:
        copy.start()
    gates = [f_ref[0:1, 0:HALF], f_ref[0:1, HALF:ROWS]]
    for half in range(2):
        gate = running_sum(jnp.where(swap == 1, gates[1 - half], gates[half]))
        rows = split_rows(gate).astype(BF16)
        qg[ROWS:PACK, HALF * half : HALF * (half + 1)] = rows
        kv[ROWS:PACK, HALF * half : HALF * (half + 1)] = rows
    for copy in copies:
        copy.wait()
    run_copies([(kv, kv_ref), (qg, qg_ref)], sems)


def totals_kernel(*refs):
    blocks, out_ref, aux, sems = refs[:8], refs[8], refs[9], refs[10]
    z, _, _, own = place_of()
    copies = []
    for at, block in enumerate(blocks):
        last = block.shape[0] - AUX
        copies.append((block.at[pl.ds(last, AUX), :], aux.at[at]))
    run_copies(copies, sems)
    table = jnp.zeros((GROUP, HALF), F32)
    for e in range(GROUP):
        row = join_rows(aux[e])
        ends = [row[:, HALF * (half + 1) - 1 : HALF * (half + 1)] for half in range(2)]
        table = table_lanes(table, near_z(z, e), own, *ends)
    out_ref[...] = table


def ids_kernel(span_ref, out_ref):
    table = jnp.zeros((GROUP, HALF), jnp.int32)
    for z in range(GROUP):
        for b in range(GROUP):
            low = slot_low(span_ref, z * GROUP + b)
            table = table_lanes(table, z, b, low, 127 - low)
    out_ref[...] = table


def run_copies(copies, sems):
    copies = [pltpu.make_async_copy(a, b, sems.at[i]) for i, (a, b) in enumerate(copies)]
    for copy in copies:
        copy.start()
    for copy in copies:
        copy.wait()


def key_copies(key_refs, ks):
    copies, at = [], 0
    for ref in key_refs:
        if ref.shape[0] == HALF + AUX:
            copies.append((ref, ks.at[at, pl.ds(HALF, HALF + AUX), :]))
        elif ref.shape[0] == HALF:
            copies.append((ref, ks.at[at, pl.ds(0, HALF), :]))
            at += 1
        else:
            copies.append((ref, ks.at[at]))
            at += 1
    return copies


def gate_columns(ks, e, columns):
    row = join_rows(ks[e, ROWS:PACK, :]) * LOG2E
    for half in range(2):
        part = row[:, HALF * half : HALF * (half + 1)]
        columns[half] = jnp.transpose(jnp.broadcast_to(part, (HALF, HALF)))


def ahead_of():
    return lax.broadcasted_iota(jnp.int32, (HALF, HALF), 0) - lax.broadcasted_iota(
        jnp.int32, (HALF, HALF), 1
    )


def lanes_of(d):
    return pl.ds(pl.multiple_of(HALF * d, HALF), HALF)


def load_queries(query_refs, y, core, qs, gates):
    copies = []
    for at, ref in enumerate(query_refs):
        d = near_column(y, core, at)
        for half in range(2):
            copies.append((ref.at[pl.ds(HALF * half, HALF), :], qs.at[half, lanes_of(d), :]))
        copies.append((ref.at[pl.ds(ROWS, AUX), :], gates.at[d]))
    return copies


def stats_kernel(scale, first, span_ref, *refs):
    z, y, core, own = place_of()
    if first:
        qt, wq = refs[:2]
        rest, refs = refs[2:], ()
        count = 3
        key_refs, (one_ref, two_ref), (ks, columns, sems) = rest[:4], rest[4:6], rest[6:]
        run_copies(key_copies(key_refs, ks), sems)
    else:
        count = 5
        query_refs, key_refs = refs[:8], refs[8:13]
        one_ref, two_ref, own_ref, qs, qt, wq, ks, columns, gates, sems = refs[13:]
        run_copies(load_queries(query_refs, y, core, qs, gates) + key_copies(key_refs, ks), sems)
        for d in range(GROUP):
            rows = slice(HALF * d, HALF * (d + 1))
            row = join_rows(gates[d]) * LOG2E
            wq[0, d : d + 1, :] = row[:, 0:HALF]
            wq[1, d : d + 1, :] = row[:, HALF:ROWS]
            for half in range(2):
                qt[0, half, :, rows] = jnp.transpose(qs[half, rows, 0:HALF])
                qt[1, half, :, rows] = jnp.transpose(qs[half, rows, HALF:ROWS])
    ahead = ahead_of()
    lows = [slot_low(span_ref, z * GROUP + d) for d in range(GROUP)]

    def tile_stats(scores, upstream):
        best = jnp.max(scores, axis=0, keepdims=True)
        factor = jnp.exp2(scores - best)
        return (
            best,
            jnp.sum(factor, axis=0, keepdims=True),
            jnp.sum(factor * upstream, axis=0, keepdims=True),
        )

    for e in range(count):
        gate_columns(ks, e, columns)
        key_span = slot_low(span_ref, near_z(z, first + e) * GROUP + own)
        key_low, value_low = ks[e, 0:HALF, 0:HALF], ks[e, 0:HALF, HALF:ROWS]
        column = columns[0]
        column2 = jnp.concatenate([column, column], 1)
        for pair in range(GROUP // 2):
            lanes = slice(ROWS * pair, ROWS * (pair + 1))
            w = jnp.concatenate([wq[1, 2 * pair + i : 2 * pair + i + 1, :] for i in range(2)], 1)
            scores = dot(key_low, qt[0, 1, :, lanes], 1, 0) * scale + (w - column2)
            upstream = dot(value_low, qt[1, 1, :, lanes], 1, 0)
            for at, row in enumerate(tile_stats(scores, upstream)):
                one_ref[e, at : at + 1, lanes] = row
        for d in range(GROUP):
            half = (key_span > lows[d]).astype(jnp.int32)
            rows, lanes = half_rows(half), slice(HALF * d, HALF * (d + 1))
            scores = dot(ks[e, rows, 0:HALF], qt[0, half, :, lanes], 1, 0) * scale + (
                wq[half, d : d + 1, :] - columns[half]
            )
            if first + e == 0:
                scores = jnp.where(ahead <= jnp.where(own == d, 0, HALF), scores, NEG)
            upstream = dot(ks[e, rows, HALF:ROWS], qt[1, half, :, lanes], 1, 0)
            for at, row in enumerate(tile_stats(scores, upstream)):
                two_ref[e, at : at + 1, lanes] = row
        if first + e == 0:
            w, lanes = wq[1, pl.ds(own, 1), :], lanes_of(own)
            scores = dot(ks[0, HALF:ROWS, 0:HALF], qt[0, 1, :, lanes], 1, 0) * scale
            scores = jnp.where(ahead <= 0, scores + (w - columns[1]), NEG)
            upstream = dot(ks[0, HALF:ROWS, HALF:ROWS], qt[1, 1, :, lanes], 1, 0)
            for at, row in enumerate(tile_stats(scores, upstream)):
                own_ref[at : at + 1, :] = row


def down(x):
    return jnp.sum(x, axis=0, keepdims=True)


def key_ranks(span_ref, z, own):
    sub = lax.broadcasted_iota(jnp.int32, (GROUP, HALF), 0)
    rank = jnp.zeros((GROUP, HALF), jnp.int32)
    for e in range(GROUP):
        rank = jnp.where(sub == e, slot_low(span_ref, near_z(z, e) * GROUP + own), rank)
    return rank


def tile_rows(near_ref, far_ref, at, lanes):
    return jnp.concatenate([near_ref[:, at, lanes], far_ref[:, at, lanes]], 0)


def merge_kernel(
    span_ref, ids_ref, t0, t1, t2, t3, near1, near2, own_ref, far1, far2, out_ref, place_ref
):
    z, y, core, own = place_of()
    ids, totals = ids_ref[...], t0[...] + t1[...] + t2[...] + t3[...]
    lows = [slot_low(span_ref, near_z(z, e) * GROUP + own) for e in range(GROUP)]
    lows += [slot_low(span_ref, z * GROUP + d) for d in range(GROUP)]
    places = {}
    for at in range(2 * GROUP):
        for half in range(2):
            span = 127 - lows[at] if half else lows[at]
            before = jnp.where(ids < span, totals, 0.0)
            place = jnp.sum(down(before), axis=1, keepdims=True) * LOG2E
            row = 2 * GROUP * (at // GROUP) + GROUP * half + at % GROUP
            places[row] = jnp.broadcast_to(place, (1, HALF))
            place_ref[row : row + 1, :] = places[row]
    key_low = jnp.concatenate([places[i] for i in range(0, 8)], 0)
    key_high = jnp.concatenate([places[i] for i in range(8, 16)], 0)
    ranks = key_ranks(span_ref, z, own)

    def finish(best, total, weighted, at, d):
        some = total > 0.0
        safe = jnp.where(some, total, 1.0)
        lse = jnp.where(some, best + jnp.log2(safe), NEG)
        delta = jnp.where(some, weighted / safe, 0.0)
        for copy in range(GROUP):
            out_ref[copy, at + d : at + d + 1, :] = lse
            out_ref[copy, at + 8 + d : at + 9 + d, :] = delta

    for d in range(GROUP):
        lanes = slice(HALF * d, HALF * (d + 1))
        one = [tile_rows(near1, far1, at, lanes) for at in range(3)]
        two = [tile_rows(near2, far2, at, lanes) for at in range(3)]
        high = ranks > lows[GROUP + d]
        query_low, query_high = places[16 + d], places[24 + d]
        first = one[0] + (query_high - key_low)
        second = two[0] + jnp.where(high, query_high - key_high, query_low - key_low)
        mine = own == d
        third = jnp.where(mine, own_ref[0:1, :], NEG)
        best = jnp.maximum(
            jnp.max(jnp.maximum(first, jnp.where(high, second, NEG)), axis=0, keepdims=True), third
        )
        first_weight = jnp.exp2(first - best)
        second_weight = jnp.where(high, jnp.exp2(second - best), 0.0)
        third_weight = jnp.where(mine, jnp.exp2(third - best), 0.0)
        sums = [
            down(one[at] * first_weight + two[at] * second_weight)
            + own_ref[at : at + 1, :] * third_weight
            for at in (1, 2)
        ]
        finish(best, sums[0], sums[1], 0, d)
        low = jnp.where(high, NEG, second)
        best = jnp.max(low, axis=0, keepdims=True)
        weight = jnp.where(high, 0.0, jnp.exp2(low - best))
        sums = [down(two[at] * weight) for at in (1, 2)]
        finish(best, sums[0], sums[1], 16, d)


def combine_kernel(
    span_ref, stats_ref, place_ref, wq_ref, near1, near2, own_ref, far1, far2, gate_ref, delta_ref, out_ref
):
    z, y, core, own = place_of()
    lses, deltas = [None, None], [None, None]
    for half, at in ((1, 0), (0, 16)):
        lse = [stats_ref[b, at : at + 8, :] for b in range(GROUP)]
        best = lse[0]
        for b in range(1, GROUP):
            best = jnp.maximum(best, lse[b])
        total = jnp.zeros((GROUP, HALF), F32)
        weighted = jnp.zeros((GROUP, HALF), F32)
        for b in range(GROUP):
            weight = jnp.exp2(lse[b] - best)
            total = total + weight
            weighted = weighted + weight * stats_ref[b, at + 8 : at + 16, :]
        lses[half] = best + jnp.log2(total)
        deltas[half] = weighted / total
        gate_ref[half] = wq_ref[half] - lses[half]
        delta_ref[half] = deltas[half]
    key_low, key_high = place_ref[0:8, :], place_ref[8:16, :]
    ranks = key_ranks(span_ref, z, own)
    sub = lax.broadcasted_iota(jnp.int32, (GROUP, HALF), 0)
    low_sum = jnp.zeros((GROUP, HALF), F32)
    high_sum = jnp.zeros((GROUP, HALF), F32)
    for d in range(GROUP):
        lanes = slice(HALF * d, HALF * (d + 1))
        one = [tile_rows(near1, far1, at, lanes) for at in range(3)]
        two = [tile_rows(near2, far2, at, lanes) for at in range(3)]
        high = ranks > slot_low(span_ref, z * GROUP + d)
        lse_low, lse_high = lses[0][d : d + 1, :], lses[1][d : d + 1, :]
        delta_low, delta_high = deltas[0][d : d + 1, :], deltas[1][d : d + 1, :]
        query_low, query_high = place_ref[16 + d : 17 + d, :], place_ref[24 + d : 25 + d, :]
        first = jnp.exp2(one[0] + (query_high - key_low) - lse_high)
        first = first * (one[2] - delta_high * one[1])
        shift = jnp.where(high, query_high - key_high - lse_high, query_low - key_low - lse_low)
        second = jnp.exp2(two[0] + shift)
        second = second * (two[2] - jnp.where(high, delta_high, delta_low) * two[1])
        third = jnp.exp2(own_ref[0:1, :] - lse_high)
        third = third * (own_ref[2:3, :] - delta_high * own_ref[1:2, :])
        low_sum = low_sum + first + jnp.where(high, 0.0, second)
        high_sum = high_sum + jnp.where(high, second, 0.0)
        high_sum = high_sum + jnp.where((sub == 0) & (own == d), third, 0.0)
    low_sum = -jnp.sum(low_sum, axis=1, keepdims=True)
    high_sum = -jnp.sum(high_sum, axis=1, keepdims=True)
    table = jnp.zeros((GROUP, HALF), F32)
    for e in range(GROUP):
        row = slice(e, e + 1)
        table = table_lanes(table, near_z(z, e), own, low_sum[row, :], high_sum[row, :])
    for copy in range(GROUP):
        out_ref[copy] = table


def beyond_kernel(span_ref, ids_ref, tables_ref, a_ref, b_ref, c_ref, out_ref, a_out, b_out, c_out):
    z, y, core, own = place_of()
    table = tables_ref[0]
    for b in range(1, GROUP):
        table = table + tables_ref[b]
    ids = ids_ref[...]
    lane = lax.broadcasted_iota(jnp.int32, (1, ROWS), 1)
    rows = []
    for e in range(GROUP):
        low = slot_low(span_ref, near_z(z, e) * GROUP + own)
        row = jnp.zeros((1, ROWS), F32)
        for half, span in ((0, low), (1, 127 - low)):
            value = jnp.sum(down(jnp.where(ids > span, table, 0.0)), axis=1, keepdims=True)
            row = jnp.where(lane == HALF * (half + 1) - 1, value, row)
        rows.append(row)
        out_ref[e : e + 1, :] = row
    for row, source, target in zip(rows[5:], (a_ref, b_ref, c_ref), (a_out, b_out, c_out)):
        last = source.shape[0] - AUX
        target[0:last, :] = source[0:last, :]
        aux = join_rows(source[last : last + AUX, :]) + row
        target[last : last + AUX, :] = split_rows(aux).astype(BF16)


def grads_kernel(scale, first, count, pieces, span_ref, qs, qt, gate_ref, delta_ref, place_ref, *refs):
    z, y, core, own = place_of()
    key_refs, refs = refs[:pieces], refs[pieces:]
    if first == 5:
        dqt, refs = refs[0], refs[1:]
        dqt[...] = jnp.zeros_like(dqt)
        outs, scratch = refs[:4], refs[4:]
    elif first == 0:
        before, beyond, dqt, refs = refs[0], refs[1], refs[2], refs[3:]
        dqt[...] = before[...]
        outs, scratch = refs[:3], refs[3:]
    else:
        before, beyond, up3, down3, up4, down4, dq_ref = refs[:7]
        outs, scratch = refs[7:9], refs[9:]
        dqt, scratch = scratch[0], scratch[1:]
        dqt[...] = before[...]
    ks, columns, pg, sems = scratch
    run_copies(key_copies(key_refs, ks), sems)
    ahead = ahead_of()
    inverse = 1.0 / math.sqrt(HALF)
    lows = [slot_low(span_ref, z * GROUP + d) for d in range(GROUP)]

    def query_gate(half, d, key_place):
        place = place_ref[pl.ds(16 + 8 * half + d, 1), :]
        return gate_ref[half, d : d + 1, :] + (place - key_place)

    for e in range(count):
        number = first + e
        gate_columns(ks, e, columns)
        key_span = slot_low(span_ref, near_z(z, number) * GROUP + own)
        key_low, value_low = ks[e, 0:HALF, 0:HALF], ks[e, 0:HALF, HALF:ROWS]
        turned = jnp.transpose(ks[e, :ROWS, 0:HALF])
        column = columns[0]
        column2 = jnp.concatenate([column, column], 1)
        place = place_ref[number : number + 1, :]
        probs1, grads1, probs2, grads2 = [], [], ([], []), ([], [])
        total = jnp.zeros((HALF, HALF), F32)
        for pair in range(GROUP // 2):
            both, lanes = (2 * pair, 2 * pair + 1), slice(ROWS * pair, ROWS * (pair + 1))
            w = jnp.concatenate([query_gate(1, d, place) for d in both], 1)
            shift = jnp.concatenate([delta_ref[1, d : d + 1, :] for d in both], 1)
            probs = jnp.exp2(dot(key_low, qt[0, 1, :, lanes], 1, 0) * scale + (w - column2))
            grads = probs * (dot(value_low, qt[1, 1, :, lanes], 1, 0) - shift)
            probs1.append(probs.astype(BF16))
            grads1.append(grads.astype(BF16))
            total = total + grads[:, 0:HALF] + grads[:, HALF:ROWS]
        pg[0] = total
        pg[1] = jnp.zeros((HALF, HALF), F32)
        chosen = []
        for d in range(GROUP):
            half = (key_span > lows[d]).astype(jnp.int32)
            rows, lanes = half_rows(half), slice(HALF * d, HALF * (d + 1))
            chosen.append(qs[half, lanes, :])
            w = query_gate(half, d, place_ref[pl.ds(8 * half + number, 1), :])
            scores = dot(ks[e, rows, 0:HALF], qt[0, half, :, lanes], 1, 0) * scale
            probs = jnp.exp2(scores + (w - columns[half]))
            if number == 0:
                probs = jnp.where(ahead <= jnp.where(own == d, 0, HALF), probs, 0.0)
            upstream = dot(ks[e, rows, HALF:ROWS], qt[1, half, :, lanes], 1, 0)
            grads = probs * (upstream - delta_ref[half, d : d + 1, :])
            pg[half] += grads
            probs, grads = probs.astype(BF16), grads.astype(BF16)
            zero = jnp.zeros_like(probs)
            for side in range(2):
                probs2[side].append(jnp.where(half == side, probs, zero))
                grads2[side].append(jnp.where(half == side, grads, zero))
        chosen = jnp.concatenate(chosen, 0)
        side_probs, side_grads = (
            [jnp.concatenate(part, 1) for part in parts] for parts in (probs2, grads2)
        )
        value_parts = dot(jnp.concatenate(side_probs, 0), chosen[:, HALF:ROWS], 1, 0)
        key_parts = dot(jnp.concatenate(side_grads, 0), chosen[:, 0:HALF], 1, 0)
        dv = [
            value_parts[0:HALF, :] + dot(jnp.concatenate(probs1, 1), qs[1, :, HALF:ROWS], 1, 0),
            value_parts[HALF:ROWS, :],
        ]
        dk = [
            key_parts[0:HALF, :] + dot(jnp.concatenate(grads1, 1), qs[1, :, 0:HALF], 1, 0),
            key_parts[HALF:ROWS, :],
        ]
        for pair in range(GROUP // 2):
            lanes = slice(ROWS * pair, ROWS * (pair + 1))
            stack = jnp.concatenate([grads1[pair], side_grads[1][:, lanes]], 0)
            dqt[1, :, lanes] += dot(turned, stack, 1, 0)
            dqt[0, :, lanes] += dot(turned[:, 0:HALF], side_grads[0][:, lanes], 1, 0)
        if number == 0:
            lanes = lanes_of(own)
            scores = dot(ks[e, HALF:ROWS, 0:HALF], qt[0, 1, :, lanes], 1, 0) * scale
            probs = jnp.exp2(scores + (gate_ref[1, pl.ds(own, 1), :] - columns[1]))
            probs = jnp.where(ahead <= 0, probs, 0.0)
            upstream = dot(ks[e, HALF:ROWS, HALF:ROWS], qt[1, 1, :, lanes], 1, 0)
            grads = probs * (upstream - delta_ref[1, pl.ds(own, 1), :])
            low_grads, block = grads.astype(BF16), qs[1, lanes_of(own), :]
            dv[1] = dv[1] + dot(probs.astype(BF16), block[:, HALF:ROWS], 1, 0)
            dk[1] = dk[1] + dot(low_grads, block[:, 0:HALF], 1, 0)
            dqt[1, :, lanes] += dot(turned[:, HALF:ROWS], low_grads, 1, 0)
            pg[1] += grads

        for half in range(2):
            rows = slice(HALF * half, HALF * (half + 1))
            key_part, value_part = dk[half] * inverse, dv[half]
            row = -down(jnp.transpose(pg[half]))
            if number < 5:
                row = row + beyond[number : number + 1, rows]
            out, base, keep_aux = outs[e], HALF * half, True
            if number == 7:
                out, base, keep_aux = outs[2 + half], 0, half == 1
            if number in (3, 4):
                arrived = (up3, down3)[number - 3]
                key_part = key_part + arrived[rows, 0:HALF].astype(F32)
                value_part = value_part + arrived[rows, HALF:ROWS].astype(F32)
                row = row + join_rows(arrived[ROWS:PACK, rows])
                if number == 3:
                    row = row + join_rows(up4[HALF : HALF + AUX, rows])
                if half == 4 - number:
                    arrived = (up4, down4)[number - 3]
                    key_part = key_part + arrived[0:HALF, 0:HALF].astype(F32)
                    value_part = value_part + arrived[0:HALF, HALF:ROWS].astype(F32)
            out[base : base + HALF, 0:HALF] = key_part.astype(BF16)
            out[base : base + HALF, HALF:ROWS] = value_part.astype(BF16)
            aux_out = outs[3] if number == 7 else out
            aux_base = HALF if number == 7 else ROWS
            aux_out[aux_base : aux_base + AUX, rows] = split_rows(row).astype(BF16)

    if first == 3:
        for d in range(GROUP):
            for half in range(2):
                part = jnp.transpose(dqt[half, :, HALF * d : HALF * (d + 1)]) * inverse
                dq_ref[d, HALF * half : HALF * (half + 1), :] = part.astype(BF16)


def final_kernel(
    span_ref, dq_parts, p0, p1, p2, p3, p4, dq_ref, dk_ref, dv_ref, f_ref
):
    z, y, core, own = place_of()
    swap = own_swap(span_ref)
    parts = (p0, p1, p2, p3, p4)
    halves = []
    for half in range(2):
        rows = slice(HALF * half, HALF * (half + 1))
        target = half_rows(jnp.bitwise_xor(half, swap))
        total = dq_parts[0, rows, :].astype(F32)
        for b in range(1, GROUP):
            total = total + dq_parts[b, rows, :].astype(F32)
        dq_ref[target, :] = total.astype(BF16)
        total = p0[rows, :].astype(F32)
        for part in parts[1:]:
            total = total + part[rows, :].astype(F32)
        total = total.astype(BF16)
        dk_ref[target, :] = total[:, 0:HALF]
        dv_ref[target, :] = total[:, HALF:ROWS]
        row = join_rows(p0[ROWS:PACK, rows])
        for part in parts[1:]:
            row = row + join_rows(part[ROWS:PACK, rows])
        total = jnp.sum(row, axis=1, keepdims=True)
        halves.append(total - running_sum(row) + row)
    for half in range(2):
        lanes = slice(HALF * half, HALF * (half + 1))
        f_ref[:, lanes] = jnp.where(swap == 1, halves[1 - half], halves[half])


def fetch(x, axis, size, offset):
    return lax.ppermute(x, axis, [((i + offset) % size, i) for i in range(size)])


def local(queries, key_vectors, value_vectors, out_grad, log_forget, span_order):
    scale = LOG2E / math.sqrt(HALF)

    def struct(shape, kind):
        return jax.ShapeDtypeStruct(shape, kind)

    block = struct((PACK, ROWS), BF16)
    table = struct((GROUP, HALF), F32)
    qg, kv = call(
        pack_kernel,
        (block, block),
        [smem] + [hbm] * 4 + [vmem],
        [pltpu.VMEM((PACK, ROWS), BF16)] * 2 + [pltpu.SemaphoreType.DMA((8,))],
        out_spec=(hbm, hbm),
        limit=62 * 1024 * 1024,
    )(span_order, queries[0], key_vectors[0], value_vectors[0], out_grad[0], log_forget)
    ids = call(ids_kernel, struct((GROUP, HALF), jnp.int32), [smem])(span_order)
    up1, down1, up2, down2 = [fetch(kv, Z, 8, o) for o in (1, -1, 2, -2)]
    mine = [qg] + [fetch(qg, Y, 4, o) for o in (1, -1, 2)]
    up3, down3 = fetch(up2, Z, 8, 1), fetch(down2, Z, 8, -1)
    theirs = [fetch(x, C, 2, 1) for x in mine]
    far_low = fetch(down2[:HALF], Z, 8, -2)
    far_high = fetch(up2[HALF:], Z, 8, 2)
    query_blocks = [x for pair in zip(mine, theirs) for x in pair]
    near_keys = [kv, up1, down1, up2, down2]
    far_keys = [up3, down3, far_high, far_low]

    totals = call(
        totals_kernel,
        table,
        [hbm] * 8,
        [pltpu.VMEM((8, AUX, ROWS), BF16), pltpu.SemaphoreType.DMA((8,))],
    )(*near_keys, *far_keys[:3])
    totals = totals + fetch(totals, C, 2, 1)
    totals = [totals] + [fetch(totals, Y, 4, o) for o in (1, -1, 2)]

    def key_scratch(count, sems, more=()):
        return [
            pltpu.VMEM((count, PACK, ROWS), BF16),
            pltpu.VMEM((2, HALF, HALF), F32),
            *more,
            pltpu.SemaphoreType.DMA((sems,)),
        ]

    def tiles(count):
        return struct((count, 3, GROUP * HALF), F32)

    gates = struct((2, GROUP, HALF), F32)
    near1, near2, own, qs, qt, wq = call(
        lambda *refs: stats_kernel(scale, 0, *refs),
        (
            tiles(5),
            tiles(5),
            struct((GROUP, HALF), F32),
            struct((2, GROUP * HALF, ROWS), BF16),
            struct((2, 2, HALF, GROUP * HALF), BF16),
            gates,
        ),
        [smem] + [hbm] * 13,
        key_scratch(5, 29, [pltpu.VMEM((GROUP, AUX, ROWS), BF16)]),
        flops=1 << 31,
    )(span_order, *query_blocks, *near_keys)
    far1, far2 = call(
        lambda *refs: stats_kernel(scale, 5, *refs),
        (tiles(3), tiles(3)),
        [smem, vmem, vmem] + [hbm] * 4,
        key_scratch(3, 4),
        flops=1 << 31,
    )(span_order, qt, wq, *far_keys)
    stats, place = call(
        merge_kernel,
        (struct((GROUP, 32, HALF), F32), struct((32, HALF), F32)),
        [smem] + [vmem] * 10,
    )(span_order, ids, *totals, near1, near2, own, far1, far2)
    stats = lax.all_to_all(stats, COLUMN, 0, 0, tiled=True)
    gate, delta, span_grads = call(
        combine_kernel,
        (gates, gates, struct((GROUP, GROUP, HALF), F32)),
        [smem] + [vmem] * 8,
    )(span_order, stats, place, wq, near1, near2, own, far1, far2)
    span_grads = lax.all_to_all(span_grads, COLUMN, 0, 0, tiled=True)
    square = pltpu.VMEM((2, HALF, HALF), F32)
    sum_t = struct((2, HALF, GROUP * HALF), F32)

    def grads(first, count, keys, more, outs, extra=()):
        return call(
            lambda *refs: grads_kernel(scale, first, count, len(keys), *refs),
            outs,
            [smem] + [vmem] * 5 + [hbm] * len(keys) + [vmem] * len(more),
            list(extra)
            + [
                pltpu.VMEM((count, PACK, ROWS), BF16),
                square,
                square,
                pltpu.SemaphoreType.DMA((len(keys),)),
            ],
            flops=1 << 31,
        )(span_order, qs, qt, gate, delta, place, *keys, *more)

    low_piece, high_piece = struct((HALF, ROWS), BF16), struct((HALF + AUX, ROWS), BF16)
    dqt, part3, part3d, part4, part4d_high = grads(
        5, 3, far_keys, [], (sum_t, block, block, low_piece, high_piece)
    )
    beyond, part3, part3d, part4d_high = call(
        beyond_kernel,
        (struct((GROUP, ROWS), F32), block, block, high_piece),
        [smem] + [vmem] * 5,
    )(span_order, ids, span_grads, part3, part3d, part4d_high)
    arrived_up3, arrived_down3 = fetch(part3, Z, 8, -1), fetch(part3d, Z, 8, 1)
    arrived_up4, arrived_down4 = fetch(part4d_high, Z, 8, -2), fetch(part4, Z, 8, 2)
    dqt, part0, part1, part1d = grads(0, 3, near_keys[:3], [dqt, beyond], (sum_t, block, block, block))
    arrived1, arrived1d = fetch(part1, Z, 8, -1), fetch(part1d, Z, 8, 1)
    dq_parts, part2, part2d = grads(
        3,
        2,
        near_keys[3:],
        [dqt, beyond, arrived_up3, arrived_down3, arrived_up4, arrived_down4],
        (struct((GROUP, ROWS, HALF), BF16), block, block),
        [pltpu.VMEM((2, HALF, GROUP * HALF), F32)],
    )
    arrived2, arrived2d = fetch(part2, Z, 8, -2), fetch(part2d, Z, 8, 2)
    dq_parts = lax.all_to_all(dq_parts, COLUMN, 0, 0, tiled=True)
    rows = struct((ROWS, HALF), BF16)
    dq, dk, dv, forget = call(
        final_kernel, (rows, rows, rows, struct((1, ROWS), F32)), [smem] + [vmem] * 6
    )(span_order, dq_parts, part0, arrived1, arrived1d, arrived2, arrived2d)
    return dq[None], dk[None], dv[None], forget


def solution(mesh):
    fine = Mesh(mesh.devices.reshape(8, 2, 2, 2, 4), ("z", "y_hi", "y_lo", "core", "head"))
    rows = ("z", "y_hi", "y_lo", "core")
    wide, thin = P("head", rows, None), P("head", rows)
    return jax.shard_map(
        local,
        mesh=fine,
        in_specs=(wide, wide, wide, wide, thin, P()),
        out_specs=(wide, wide, wide, thin),
        check_vma=False,
    )
```

```python
import math

import jax
import jax.numpy as jnp
from jax import lax
from jax.experimental import pallas as pl
from jax.experimental.pallas import tpu as pltpu
from jax.sharding import Mesh, PartitionSpec as P

F32 = jnp.float32
BF16 = jnp.bfloat16
LOG2E = 1.4426950408889634
NEG = -1e30
GROUP = 8
HALF = 128
ROWS = 256
AUX = 16
PACK = ROWS + AUX
NEAR = (0, 1, -1, 2, -2, 3, -3, 4)
Z, Y, C = "z", ("y_hi", "y_lo"), "core"
COLUMN = ("y_hi", "y_lo", "core")
VMEM_LIMIT = 20 * 1024 * 1024
vmem = pl.BlockSpec(memory_space=pltpu.VMEM)
smem = pl.BlockSpec(memory_space=pltpu.SMEM)
hbm = pl.BlockSpec(memory_space=pl.ANY)


def call(kernel, outs, in_specs, scratch=(), flops=0, out_spec=None, limit=VMEM_LIMIT):
    return pl.pallas_call(
        kernel,
        out_shape=outs,
        in_specs=in_specs,
        out_specs=out_spec or jax.tree.map(lambda _: vmem, outs),
        scratch_shapes=list(scratch),
        compiler_params=pltpu.CompilerParams(vmem_limit_bytes=limit),
        cost_estimate=pl.CostEstimate(flops=flops, bytes_accessed=4 << 20, transcendentals=0),
    )


def dot(a, b, ca, cb):
    return lax.dot_general(a, b, (((ca,), (cb,)), ((), ())), preferred_element_type=F32)


def split_rows(row, first=0):
    high = row.astype(BF16).astype(F32)
    middle = (row - high).astype(BF16).astype(F32)
    low = row - high - middle
    at = lax.broadcasted_iota(jnp.int32, (AUX, row.shape[1]), 0) - first
    return jnp.where(at == 0, high, jnp.where(at == 1, middle, jnp.where(at == 2, low, 0.0)))


def join_rows(rows, first=0):
    rows = rows.astype(F32)
    return rows[first : first + 1] + rows[first + 1 : first + 2] + rows[first + 2 : first + 3]


def running_sum(row):
    lane = lax.broadcasted_iota(jnp.int32, row.shape, 1)
    step = 1
    while step < HALF:
        row = row + jnp.where(lane >= step, pltpu.roll(row, step, 1), 0.0)
        step *= 2
    return row


def place_of():
    z, y, core = lax.axis_index(Z), lax.axis_index("y_hi") * 2 + lax.axis_index("y_lo"), lax.axis_index(C)
    return z, y, core, y * 2 + core


def slot_low(span_ref, slot):
    return jnp.minimum(span_ref[2 * slot], span_ref[2 * slot + 1])


def own_swap(span_ref):
    z, _, _, column = place_of()
    slot = 2 * (z * GROUP + column)
    return (span_ref[slot] > span_ref[slot + 1]).astype(jnp.int32)


def near_z(z, e):
    return lax.rem(z + (NEAR[e] + GROUP), GROUP)


def near_column(y, core, at):
    offset, other = (0, 1, 3, 2)[at // 2], at % 2
    return lax.rem(y + offset, 4) * 2 + (1 - core if other else core)


def half_rows(half):
    return pl.ds(pl.multiple_of(HALF * half, HALF), HALF)


def table_lanes(table, z, own, low, high):
    sub = lax.broadcasted_iota(jnp.int32, (GROUP, HALF), 0)
    lane = lax.broadcasted_iota(jnp.int32, (GROUP, HALF), 1)
    table = jnp.where((sub == z) & (lane == 2 * own), low, table)
    return jnp.where((sub == z) & (lane == 2 * own + 1), high, table)


def pack_kernel(
    span_ref, q_ref, k_ref, v_ref, g_ref, f_ref, qg_ref, kv_ref, ids_ref, qg, kv, sems
):
    swap = own_swap(span_ref)
    copies = []
    for half in range(2):
        source = half_rows(jnp.bitwise_xor(half, swap))
        target = pl.ds(HALF * half, HALF)
        for ref, out, lanes in (
            (k_ref, kv, pl.ds(0, HALF)),
            (v_ref, kv, pl.ds(HALF, HALF)),
            (q_ref, qg, pl.ds(0, HALF)),
            (g_ref, qg, pl.ds(HALF, HALF)),
        ):
            copies.append((ref.at[source, :], out.at[target, lanes]))
    copies = [pltpu.make_async_copy(a, b, sems.at[i]) for i, (a, b) in enumerate(copies)]
    for copy in copies:
        copy.start()
    gates = [f_ref[0:1, 0:HALF], f_ref[0:1, HALF:ROWS]]
    gates = [jnp.where(swap == 1, gates[1 - half], gates[half]) for half in range(2)]
    gates = running_sum(jnp.concatenate(gates, 0))
    for half in range(2):
        rows = split_rows(gates[half : half + 1, :]).astype(BF16)
        qg[ROWS:PACK, HALF * half : HALF * (half + 1)] = rows
        kv[ROWS:PACK, HALF * half : HALF * (half + 1)] = rows
    ids = jnp.zeros((GROUP, HALF), jnp.int32)
    for z in range(GROUP):
        for b in range(GROUP):
            low = slot_low(span_ref, z * GROUP + b)
            ids = table_lanes(ids, z, b, low, 127 - low)
    ids_ref[...] = ids
    for copy in copies:
        copy.wait()
    run_copies([(kv, kv_ref), (qg, qg_ref)], sems)


def totals_kernel(*refs):
    blocks, out_ref, aux, sems = refs[:8], refs[8], refs[9], refs[10]
    z, _, _, own = place_of()
    copies = []
    for at, block in enumerate(blocks):
        last = block.shape[0] - AUX
        copies.append((block.at[pl.ds(last, AUX), :], aux.at[at]))
    run_copies(copies, sems)
    table = jnp.zeros((GROUP, HALF), F32)
    for e in range(GROUP):
        row = join_rows(aux[e])
        ends = [row[:, HALF * (half + 1) - 1 : HALF * (half + 1)] for half in range(2)]
        table = table_lanes(table, near_z(z, e), own, *ends)
    out_ref[...] = table


def totals_kernel(*refs):
    blocks, out_ref, aux, sems = refs[:8], refs[8], refs[9], refs[10]
    z, _, _, own = place_of()
    copies = []
    for at, block in enumerate(blocks):
        last = block.shape[0] - AUX
        copies.append((block.at[pl.ds(last, AUX), :], aux.at[at]))
    run_copies(copies, sems)
    table = jnp.zeros((GROUP, HALF), F32)
    for e in range(GROUP):
        row = join_rows(aux[e])
        ends = [row[:, HALF * (half + 1) - 1 : HALF * (half + 1)] for half in range(2)]
        table = table_lanes(table, near_z(z, e), own, *ends)
    out_ref[...] = table


def ids_kernel(span_ref, out_ref):
    table = jnp.zeros((GROUP, HALF), jnp.int32)
    for z in range(GROUP):
        for b in range(GROUP):
            low = slot_low(span_ref, z * GROUP + b)
            table = table_lanes(table, z, b, low, 127 - low)
    out_ref[...] = table


def run_copies(copies, sems):
    copies = [pltpu.make_async_copy(a, b, sems.at[i]) for i, (a, b) in enumerate(copies)]
    for copy in copies:
        copy.start()
    for copy in copies:
        copy.wait()


def whole_keys(key_refs, last):
    if len(key_refs) == 4:
        last[HALF:PACK, :] = key_refs[2][...]
        last[0:HALF, :] = key_refs[3][...]
        return [*key_refs[:2], last]
    return key_refs


def gate_columns(ks, e, columns):
    row = join_rows(ks[e][ROWS:PACK, :]) * LOG2E
    for half in range(2):
        part = row[:, HALF * half : HALF * (half + 1)]
        columns[half] = jnp.transpose(jnp.broadcast_to(part, (HALF, HALF)))


def ahead_of():
    return lax.broadcasted_iota(jnp.int32, (HALF, HALF), 0) - lax.broadcasted_iota(
        jnp.int32, (HALF, HALF), 1
    )


def lanes_of(d):
    return pl.ds(pl.multiple_of(HALF * d, HALF), HALF)


def load_queries(query_refs, y, core, qs, gates):
    copies = []
    for at, ref in enumerate(query_refs):
        d = near_column(y, core, at)
        for half in range(2):
            copies.append((ref.at[pl.ds(HALF * half, HALF), :], qs.at[half, lanes_of(d), :]))
        copies.append((ref.at[pl.ds(ROWS, AUX), :], gates.at[d]))
    return copies


def stats_kernel(scale, first, span_ref, *refs):
    z, y, core, own = place_of()
    if first:
        qt, wq = refs[:2]
        rest, refs = refs[2:], ()
        count = 3
        key_refs, (one_ref, two_ref), (last, columns) = rest[:4], rest[4:6], rest[6:]
        ks = whole_keys(key_refs, last)
    else:
        count = 5
        query_refs, ks = refs[:8], refs[8:13]
        one_ref, two_ref, own_ref, qs, qt, wq, columns, gates, sems = refs[13:]
        run_copies(load_queries(query_refs, y, core, qs, gates), sems)
        for d in range(GROUP):
            rows = slice(HALF * d, HALF * (d + 1))
            row = join_rows(gates[d]) * LOG2E
            wq[0, d : d + 1, :] = row[:, 0:HALF]
            wq[1, d : d + 1, :] = row[:, HALF:ROWS]
            for half in range(2):
                qt[0, half, :, rows] = jnp.transpose(qs[half, rows, 0:HALF])
                qt[1, half, :, rows] = jnp.transpose(qs[half, rows, HALF:ROWS])
    ahead = ahead_of()
    lows = [slot_low(span_ref, z * GROUP + d) for d in range(GROUP)]

    def tile_stats(scores, upstream):
        best = jnp.max(scores, axis=0, keepdims=True)
        factor = jnp.exp2(scores - best)
        return (
            best,
            jnp.sum(factor, axis=0, keepdims=True),
            jnp.sum(factor * upstream, axis=0, keepdims=True),
        )

    for e in range(count):
        gate_columns(ks, e, columns)
        key_span = slot_low(span_ref, near_z(z, first + e) * GROUP + own)
        key_low, value_low = ks[e][0:HALF, 0:HALF], ks[e][0:HALF, HALF:ROWS]
        column = columns[0]
        column2 = jnp.concatenate([column, column], 1)
        for pair in range(GROUP // 2):
            lanes = slice(ROWS * pair, ROWS * (pair + 1))
            w = jnp.concatenate([wq[1, 2 * pair + i : 2 * pair + i + 1, :] for i in range(2)], 1)
            scores = dot(key_low, qt[0, 1, :, lanes], 1, 0) * scale + (w - column2)
            upstream = dot(value_low, qt[1, 1, :, lanes], 1, 0)
            for at, row in enumerate(tile_stats(scores, upstream)):
                one_ref[e, at : at + 1, lanes] = row
        for d in range(GROUP):
            half = (key_span > lows[d]).astype(jnp.int32)
            rows, lanes = half_rows(half), slice(HALF * d, HALF * (d + 1))
            scores = dot(ks[e][rows, 0:HALF], qt[0, half, :, lanes], 1, 0) * scale + (
                wq[half, d : d + 1, :] - columns[half]
            )
            if first + e == 0:
                scores = jnp.where(ahead <= jnp.where(own == d, 0, HALF), scores, NEG)
            upstream = dot(ks[e][rows, HALF:ROWS], qt[1, half, :, lanes], 1, 0)
            for at, row in enumerate(tile_stats(scores, upstream)):
                two_ref[e, at : at + 1, lanes] = row
        if first + e == 0:
            w, lanes = wq[1, pl.ds(own, 1), :], lanes_of(own)
            scores = dot(ks[0][HALF:ROWS, 0:HALF], qt[0, 1, :, lanes], 1, 0) * scale
            scores = jnp.where(ahead <= 0, scores + (w - columns[1]), NEG)
            upstream = dot(ks[0][HALF:ROWS, HALF:ROWS], qt[1, 1, :, lanes], 1, 0)
            for at, row in enumerate(tile_stats(scores, upstream)):
                own_ref[at : at + 1, :] = row


def down(x):
    return jnp.sum(x, axis=0, keepdims=True)


def key_ranks(span_ref, z, own):
    sub = lax.broadcasted_iota(jnp.int32, (GROUP, HALF), 0)
    rank = jnp.zeros((GROUP, HALF), jnp.int32)
    for e in range(GROUP):
        rank = jnp.where(sub == e, slot_low(span_ref, near_z(z, e) * GROUP + own), rank)
    return rank


def tile_rows(near_ref, far_ref, at, lanes):
    return jnp.concatenate([near_ref[:, at, lanes], far_ref[:, at, lanes]], 0)


def merge_kernel(
    span_ref, ids_ref, t0, t1, t2, t3, near1, near2, own_ref, far1, far2, out_ref, place_ref
):
    z, y, core, own = place_of()
    ids, totals = ids_ref[...], t0[...] + t1[...] + t2[...] + t3[...]
    lows = [slot_low(span_ref, near_z(z, e) * GROUP + own) for e in range(GROUP)]
    lows += [slot_low(span_ref, z * GROUP + d) for d in range(GROUP)]
    places = {}
    for at in range(2 * GROUP):
        for half in range(2):
            span = 127 - lows[at] if half else lows[at]
            before = jnp.where(ids < span, totals, 0.0)
            place = jnp.sum(down(before), axis=1, keepdims=True) * LOG2E
            row = 2 * GROUP * (at // GROUP) + GROUP * half + at % GROUP
            places[row] = jnp.broadcast_to(place, (1, HALF))
            place_ref[row : row + 1, :] = places[row]
    key_low = jnp.concatenate([places[i] for i in range(0, 8)], 0)
    key_high = jnp.concatenate([places[i] for i in range(8, 16)], 0)
    ranks = key_ranks(span_ref, z, own)

    def finish(best, total, weighted, at, d):
        some = total > 0.0
        safe = jnp.where(some, total, 1.0)
        lse = jnp.where(some, best + jnp.log2(safe), NEG)
        delta = jnp.where(some, weighted / safe, 0.0)
        for copy in range(GROUP):
            out_ref[copy, at + d : at + d + 1, :] = lse
            out_ref[copy, at + 8 + d : at + 9 + d, :] = delta

    for d in range(GROUP):
        lanes = slice(HALF * d, HALF * (d + 1))
        one = [tile_rows(near1, far1, at, lanes) for at in range(3)]
        two = [tile_rows(near2, far2, at, lanes) for at in range(3)]
        high = ranks > lows[GROUP + d]
        query_low, query_high = places[16 + d], places[24 + d]
        first = one[0] + (query_high - key_low)
        second = two[0] + jnp.where(high, query_high - key_high, query_low - key_low)
        mine = own == d
        third = jnp.where(mine, own_ref[0:1, :], NEG)
        best = jnp.maximum(
            jnp.max(jnp.maximum(first, jnp.where(high, second, NEG)), axis=0, keepdims=True), third
        )
        first_weight = jnp.exp2(first - best)
        second_weight = jnp.where(high, jnp.exp2(second - best), 0.0)
        third_weight = jnp.where(mine, jnp.exp2(third - best), 0.0)
        sums = [
            down(one[at] * first_weight + two[at] * second_weight)
            + own_ref[at : at + 1, :] * third_weight
            for at in (1, 2)
        ]
        finish(best, sums[0], sums[1], 0, d)
        low = jnp.where(high, NEG, second)
        best = jnp.max(low, axis=0, keepdims=True)
        weight = jnp.where(high, 0.0, jnp.exp2(low - best))
        sums = [down(two[at] * weight) for at in (1, 2)]
        finish(best, sums[0], sums[1], 16, d)


def combine_kernel(
    span_ref, stats_ref, place_ref, wq_ref, near1, near2, own_ref, far1, far2, gate_ref, delta_ref, out_ref
):
    z, y, core, own = place_of()
    lses, deltas = [None, None], [None, None]
    for half, at in ((1, 0), (0, 16)):
        lse = [stats_ref[b, at : at + 8, :] for b in range(GROUP)]
        best = lse[0]
        for b in range(1, GROUP):
            best = jnp.maximum(best, lse[b])
        total = jnp.zeros((GROUP, HALF), F32)
        weighted = jnp.zeros((GROUP, HALF), F32)
        for b in range(GROUP):
            weight = jnp.exp2(lse[b] - best)
            total = total + weight
            weighted = weighted + weight * stats_ref[b, at + 8 : at + 16, :]
        lses[half] = best + jnp.log2(total)
        deltas[half] = weighted / total
        gate_ref[half] = wq_ref[half] - lses[half]
        delta_ref[half] = deltas[half]
    key_low, key_high = place_ref[0:8, :], place_ref[8:16, :]
    ranks = key_ranks(span_ref, z, own)
    sub = lax.broadcasted_iota(jnp.int32, (GROUP, HALF), 0)
    low_sum = jnp.zeros((GROUP, HALF), F32)
    high_sum = jnp.zeros((GROUP, HALF), F32)
    for d in range(GROUP):
        lanes = slice(HALF * d, HALF * (d + 1))
        one = [tile_rows(near1, far1, at, lanes) for at in range(3)]
        two = [tile_rows(near2, far2, at, lanes) for at in range(3)]
        high = ranks > slot_low(span_ref, z * GROUP + d)
        lse_low, lse_high = lses[0][d : d + 1, :], lses[1][d : d + 1, :]
        delta_low, delta_high = deltas[0][d : d + 1, :], deltas[1][d : d + 1, :]
        query_low, query_high = place_ref[16 + d : 17 + d, :], place_ref[24 + d : 25 + d, :]
        first = jnp.exp2(one[0] + (query_high - key_low) - lse_high)
        first = first * (one[2] - delta_high * one[1])
        shift = jnp.where(high, query_high - key_high - lse_high, query_low - key_low - lse_low)
        second = jnp.exp2(two[0] + shift)
        second = second * (two[2] - jnp.where(high, delta_high, delta_low) * two[1])
        third = jnp.exp2(own_ref[0:1, :] - lse_high)
        third = third * (own_ref[2:3, :] - delta_high * own_ref[1:2, :])
        low_sum = low_sum + first + jnp.where(high, 0.0, second)
        high_sum = high_sum + jnp.where(high, second, 0.0)
        high_sum = high_sum + jnp.where((sub == 0) & (own == d), third, 0.0)
    low_sum = -jnp.sum(low_sum, axis=1, keepdims=True)
    high_sum = -jnp.sum(high_sum, axis=1, keepdims=True)
    table = jnp.zeros((GROUP, HALF), F32)
    for e in range(GROUP):
        row = slice(e, e + 1)
        table = table_lanes(table, near_z(z, e), own, low_sum[row, :], high_sum[row, :])
    for copy in range(GROUP):
        out_ref[copy] = table


def beyond_kernel(span_ref, ids_ref, tables_ref, a_ref, b_ref, c_ref, out_ref, a_out, b_out, c_out):
    z, y, core, own = place_of()
    table = tables_ref[0]
    for b in range(1, GROUP):
        table = table + tables_ref[b]
    ids = ids_ref[...]
    lane = lax.broadcasted_iota(jnp.int32, (1, ROWS), 1)
    rows = []
    for e in range(GROUP):
        low = slot_low(span_ref, near_z(z, e) * GROUP + own)
        row = jnp.zeros((1, ROWS), F32)
        for half, span in ((0, low), (1, 127 - low)):
            value = jnp.sum(down(jnp.where(ids > span, table, 0.0)), axis=1, keepdims=True)
            row = jnp.where(lane == HALF * (half + 1) - 1, value, row)
        rows.append(row)
        out_ref[e : e + 1, :] = row
    for row, source, target in zip(rows[5:], (a_ref, b_ref, c_ref), (a_out, b_out, c_out)):
        last = source.shape[0] - AUX
        target[0:last, :] = source[0:last, :]
        aux = join_rows(source[last : last + AUX, :]) + row
        target[last : last + AUX, :] = split_rows(aux).astype(BF16)


def grads_kernel(scale, first, count, pieces, span_ref, qs, qt, gate_ref, delta_ref, place_ref, *refs):
    z, y, core, own = place_of()
    key_refs, refs = refs[:pieces], refs[pieces:]
    if first == 5:
        dqt_out, refs = refs[0], refs[1:]
        outs, scratch = refs[:4], refs[4:]
        dqt, scratch = scratch[0], scratch[1:]
        dqt[...] = jnp.zeros_like(dqt)
    elif first == 0:
        before, beyond, dqt_out, refs = refs[0], refs[1], refs[2], refs[3:]
        outs, scratch = refs[:3], refs[3:]
        dqt, scratch = scratch[0], scratch[1:]
        dqt[...] = before[...].astype(F32)
    else:
        before, beyond, up3, down3, up4, down4, dq_ref = refs[:7]
        outs, scratch = refs[7:9], refs[9:]
        dqt, scratch = scratch[0], scratch[1:]
        dqt[...] = before[...].astype(F32)
    last, columns, pg = scratch
    ks = whole_keys(key_refs, last)
    ahead = ahead_of()
    inverse = 1.0 / math.sqrt(HALF)
    lows = [slot_low(span_ref, z * GROUP + d) for d in range(GROUP)]

    def query_gate(half, d, key_place):
        place = place_ref[pl.ds(16 + 8 * half + d, 1), :]
        return gate_ref[half, d : d + 1, :] + (place - key_place)

    for e in range(count):
        number = first + e
        gate_columns(ks, e, columns)
        key_span = slot_low(span_ref, near_z(z, number) * GROUP + own)
        key_low, value_low = ks[e][0:HALF, 0:HALF], ks[e][0:HALF, HALF:ROWS]
        turned = jnp.transpose(ks[e][0:ROWS, 0:HALF])
        column = columns[0]
        column2 = jnp.concatenate([column, column], 1)
        place = place_ref[number : number + 1, :]
        probs1, grads1, probs2, grads2 = [], [], ([], []), ([], [])
        total = jnp.zeros((HALF, HALF), F32)
        for pair in range(GROUP // 2):
            both, lanes = (2 * pair, 2 * pair + 1), slice(ROWS * pair, ROWS * (pair + 1))
            w = jnp.concatenate([query_gate(1, d, place) for d in both], 1)
            shift = jnp.concatenate([delta_ref[1, d : d + 1, :] for d in both], 1)
            probs = jnp.exp2(dot(key_low, qt[0, 1, :, lanes], 1, 0) * scale + (w - column2))
            grads = probs * (dot(value_low, qt[1, 1, :, lanes], 1, 0) - shift)
            probs1.append(probs.astype(BF16))
            grads1.append(grads.astype(BF16))
            total = total + grads[:, 0:HALF] + grads[:, HALF:ROWS]
        pg[0] = total
        pg[1] = jnp.zeros((HALF, HALF), F32)
        chosen = []
        for d in range(GROUP):
            half = (key_span > lows[d]).astype(jnp.int32)
            rows, lanes = half_rows(half), slice(HALF * d, HALF * (d + 1))
            chosen.append(qs[half, lanes, :])
            w = query_gate(half, d, place_ref[pl.ds(8 * half + number, 1), :])
            scores = dot(ks[e][rows, 0:HALF], qt[0, half, :, lanes], 1, 0) * scale
            probs = jnp.exp2(scores + (w - columns[half]))
            if number == 0:
                probs = jnp.where(ahead <= jnp.where(own == d, 0, HALF), probs, 0.0)
            upstream = dot(ks[e][rows, HALF:ROWS], qt[1, half, :, lanes], 1, 0)
            grads = probs * (upstream - delta_ref[half, d : d + 1, :])
            pg[half] += grads
            probs, grads = probs.astype(BF16), grads.astype(BF16)
            zero = jnp.zeros_like(probs)
            for side in range(2):
                probs2[side].append(jnp.where(half == side, probs, zero))
                grads2[side].append(jnp.where(half == side, grads, zero))
        chosen = jnp.concatenate(chosen, 0)
        side_probs, side_grads = (
            [jnp.concatenate(part, 1) for part in parts] for parts in (probs2, grads2)
        )
        value_parts = dot(jnp.concatenate(side_probs, 0), chosen[:, HALF:ROWS], 1, 0)
        key_parts = dot(jnp.concatenate(side_grads, 0), chosen[:, 0:HALF], 1, 0)
        dv = [
            value_parts[0:HALF, :] + dot(jnp.concatenate(probs1, 1), qs[1, :, HALF:ROWS], 1, 0),
            value_parts[HALF:ROWS, :],
        ]
        dk = [
            key_parts[0:HALF, :] + dot(jnp.concatenate(grads1, 1), qs[1, :, 0:HALF], 1, 0),
            key_parts[HALF:ROWS, :],
        ]
        for pair in range(GROUP // 2):
            lanes = slice(ROWS * pair, ROWS * (pair + 1))
            stack = jnp.concatenate([grads1[pair], side_grads[1][:, lanes]], 0)
            dqt[1, :, lanes] += dot(turned, stack, 1, 0)
            dqt[0, :, lanes] += dot(turned[:, 0:HALF], side_grads[0][:, lanes], 1, 0)
        if number == 0:
            lanes = lanes_of(own)
            scores = dot(ks[e][HALF:ROWS, 0:HALF], qt[0, 1, :, lanes], 1, 0) * scale
            probs = jnp.exp2(scores + (gate_ref[1, pl.ds(own, 1), :] - columns[1]))
            probs = jnp.where(ahead <= 0, probs, 0.0)
            upstream = dot(ks[e][HALF:ROWS, HALF:ROWS], qt[1, 1, :, lanes], 1, 0)
            grads = probs * (upstream - delta_ref[1, pl.ds(own, 1), :])
            low_grads, block = grads.astype(BF16), qs[1, lanes_of(own), :]
            dv[1] = dv[1] + dot(probs.astype(BF16), block[:, HALF:ROWS], 1, 0)
            dk[1] = dk[1] + dot(low_grads, block[:, 0:HALF], 1, 0)
            dqt[1, :, lanes] += dot(turned[:, HALF:ROWS], low_grads, 1, 0)
            pg[1] += grads

        for half in range(2):
            rows = slice(HALF * half, HALF * (half + 1))
            key_part, value_part = dk[half] * inverse, dv[half]
            row = -down(jnp.transpose(pg[half]))
            if number < 5:
                row = row + beyond[number : number + 1, rows]
            out, base, keep_aux = outs[e], HALF * half, True
            if number == 7:
                out, base, keep_aux = outs[2 + half], 0, half == 1
            if number in (3, 4):
                arrived = (up3, down3)[number - 3]
                key_part = key_part + arrived[rows, 0:HALF].astype(F32)
                value_part = value_part + arrived[rows, HALF:ROWS].astype(F32)
                row = row + join_rows(arrived[ROWS:PACK, rows])
                if number == 3:
                    row = row + join_rows(up4[HALF : HALF + AUX, rows])
                if half == 4 - number:
                    arrived = (up4, down4)[number - 3]
                    key_part = key_part + arrived[0:HALF, 0:HALF].astype(F32)
                    value_part = value_part + arrived[0:HALF, HALF:ROWS].astype(F32)
            out[base : base + HALF, 0:HALF] = key_part.astype(BF16)
            out[base : base + HALF, HALF:ROWS] = value_part.astype(BF16)
            aux_out = outs[3] if number == 7 else out
            aux_base = HALF if number == 7 else ROWS
            aux_out[aux_base : aux_base + AUX, rows] = split_rows(row).astype(BF16)

    if first != 3:
        dqt_out[...] = dqt[...].astype(BF16)
    else:
        for d in range(GROUP):
            for half in range(2):
                part = jnp.transpose(dqt[half, :, HALF * d : HALF * (d + 1)]) * inverse
                dq_ref[d, HALF * half : HALF * (half + 1), :] = part.astype(BF16)


def final_kernel(
    span_ref, dq_parts, p0, p1, p2, p3, p4, dq_ref, dk_ref, dv_ref, f_ref
):
    z, y, core, own = place_of()
    swap = own_swap(span_ref)
    parts = (p0, p1, p2, p3, p4)
    halves = []
    for half in range(2):
        rows = slice(HALF * half, HALF * (half + 1))
        target = half_rows(jnp.bitwise_xor(half, swap))
        total = dq_parts[0, rows, :].astype(F32)
        for b in range(1, GROUP):
            total = total + dq_parts[b, rows, :].astype(F32)
        dq_ref[target, :] = total.astype(BF16)
        total = p0[rows, :].astype(F32)
        for part in parts[1:]:
            total = total + part[rows, :].astype(F32)
        total = total.astype(BF16)
        dk_ref[target, :] = total[:, 0:HALF]
        dv_ref[target, :] = total[:, HALF:ROWS]
        row = join_rows(p0[ROWS:PACK, rows])
        for part in parts[1:]:
            row = row + join_rows(part[ROWS:PACK, rows])
        halves.append(row)
    both = jnp.concatenate(halves, 0)
    both = jnp.sum(both, axis=1, keepdims=True) - running_sum(both) + both
    for half in range(2):
        lanes = slice(HALF * half, HALF * (half + 1))
        f_ref[:, lanes] = jnp.where(swap == 1, both[1 - half : 2 - half, :], both[half : half + 1, :])


def fetch(x, axis, size, offset):
    return lax.ppermute(x, axis, [((i + offset) % size, i) for i in range(size)])


def local(queries, key_vectors, value_vectors, out_grad, log_forget, span_order):
    scale = LOG2E / math.sqrt(HALF)

    def struct(shape, kind):
        return jax.ShapeDtypeStruct(shape, kind)

    block = struct((PACK, ROWS), BF16)
    table = struct((GROUP, HALF), F32)
    qg, kv, ids = call(
        pack_kernel,
        (block, block, struct((GROUP, HALF), jnp.int32)),
        [smem] + [hbm] * 4 + [vmem],
        [pltpu.VMEM((PACK, ROWS), BF16)] * 2 + [pltpu.SemaphoreType.DMA((8,))],
        out_spec=(hbm, hbm, vmem),
        limit=62 * 1024 * 1024,
    )(span_order, queries[0], key_vectors[0], value_vectors[0], out_grad[0], log_forget)
    up1, down1, up2, down2 = [fetch(kv, Z, 8, o) for o in (1, -1, 2, -2)]
    mine = [qg] + [fetch(qg, Y, 4, o) for o in (1, -1, 2)]
    up3, down3 = fetch(up2, Z, 8, 1), fetch(down2, Z, 8, -1)
    theirs = [fetch(x, C, 2, 1) for x in mine]
    far_low = fetch(down2[:HALF], Z, 8, -2)
    far_high = fetch(up2[HALF:], Z, 8, 2)
    query_blocks = [x for pair in zip(mine, theirs) for x in pair]
    near_keys = [kv, up1, down1, up2, down2]
    far_keys = [up3, down3, far_high, far_low]

    totals = call(
        totals_kernel,
        table,
        [hbm] * 8,
        [pltpu.VMEM((8, AUX, ROWS), BF16), pltpu.SemaphoreType.DMA((8,))],
    )(*near_keys, *far_keys[:3])
    totals = totals + fetch(totals, C, 2, 1)
    totals = [totals] + [fetch(totals, Y, 4, o) for o in (1, -1, 2)]

    def tiles(count):
        return struct((count, 3, GROUP * HALF), F32)

    gates = struct((2, GROUP, HALF), F32)
    near1, near2, own, qs, qt, wq = call(
        lambda *refs: stats_kernel(scale, 0, *refs),
        (
            tiles(5),
            tiles(5),
            struct((GROUP, HALF), F32),
            struct((2, GROUP * HALF, ROWS), BF16),
            struct((2, 2, HALF, GROUP * HALF), BF16),
            gates,
        ),
        [smem] + [hbm] * 8 + [vmem] * 5,
        [
            pltpu.VMEM((2, HALF, HALF), F32),
            pltpu.VMEM((GROUP, AUX, ROWS), BF16),
            pltpu.SemaphoreType.DMA((24,)),
        ],
        flops=1 << 31,
    )(span_order, *query_blocks, *near_keys)
    far1, far2 = call(
        lambda *refs: stats_kernel(scale, 5, *refs),
        (tiles(3), tiles(3)),
        [smem] + [vmem] * 6,
        [pltpu.VMEM((PACK, ROWS), BF16), pltpu.VMEM((2, HALF, HALF), F32)],
        flops=1 << 31,
    )(span_order, qt, wq, *far_keys)
    stats, place = call(
        merge_kernel,
        (struct((GROUP, 32, HALF), F32), struct((32, HALF), F32)),
        [smem] + [vmem] * 10,
    )(span_order, ids, *totals, near1, near2, own, far1, far2)
    stats = lax.all_to_all(stats, COLUMN, 0, 0, tiled=True)
    gate, delta, span_grads = call(
        combine_kernel,
        (gates, gates, struct((GROUP, GROUP, HALF), F32)),
        [smem] + [vmem] * 8,
    )(span_order, stats, place, wq, near1, near2, own, far1, far2)
    span_grads = lax.all_to_all(span_grads, COLUMN, 0, 0, tiled=True)
    square = pltpu.VMEM((2, HALF, HALF), F32)
    sum_t = struct((2, HALF, GROUP * HALF), BF16)

    def grads(first, count, keys, more, outs):
        return call(
            lambda *refs: grads_kernel(scale, first, count, len(keys), *refs),
            outs,
            [smem] + [vmem] * (5 + len(keys) + len(more)),
            [
                pltpu.VMEM((2, HALF, GROUP * HALF), F32),
                pltpu.VMEM((PACK, ROWS), BF16),
                square,
                square,
            ],
            flops=1 << 31,
        )(span_order, qs, qt, gate, delta, place, *keys, *more)

    low_piece, high_piece = struct((HALF, ROWS), BF16), struct((HALF + AUX, ROWS), BF16)
    dqt, part3, part3d, part4, part4d_high = grads(
        5, 3, far_keys, [], (sum_t, block, block, low_piece, high_piece)
    )
    beyond, part3, part3d, part4d_high = call(
        beyond_kernel,
        (struct((GROUP, ROWS), F32), block, block, high_piece),
        [smem] + [vmem] * 5,
    )(span_order, ids, span_grads, part3, part3d, part4d_high)
    arrived_up3, arrived_down3 = fetch(part3, Z, 8, -1), fetch(part3d, Z, 8, 1)
    arrived_up4, arrived_down4 = fetch(part4d_high, Z, 8, -2), fetch(part4, Z, 8, 2)
    dqt, part0, part1, part1d = grads(0, 3, near_keys[:3], [dqt, beyond], (sum_t, block, block, block))
    arrived1, arrived1d = fetch(part1, Z, 8, -1), fetch(part1d, Z, 8, 1)
    dq_parts, part2, part2d = grads(
        3,
        2,
        near_keys[3:],
        [dqt, beyond, arrived_up3, arrived_down3, arrived_up4, arrived_down4],
        (struct((GROUP, ROWS, HALF), BF16), block, block),
    )
    arrived2, arrived2d = fetch(part2, Z, 8, -2), fetch(part2d, Z, 8, 2)
    dq_parts = lax.all_to_all(dq_parts, COLUMN, 0, 0, tiled=True)
    rows = struct((ROWS, HALF), BF16)
    dq, dk, dv, forget = call(
        final_kernel, (rows, rows, rows, struct((1, ROWS), F32)), [smem] + [vmem] * 6
    )(span_order, dq_parts, part0, arrived1, arrived1d, arrived2, arrived2d)
    return dq[None], dk[None], dv[None], forget


def solution(mesh):
    fine = Mesh(mesh.devices.reshape(8, 2, 2, 2, 4), ("z", "y_hi", "y_lo", "core", "head"))
    rows = ("z", "y_hi", "y_lo", "core")
    wide, thin = P("head", rows, None), P("head", rows)
    return jax.shard_map(
        local,
        mesh=fine,
        in_specs=(wide, wide, wide, wide, thin, P()),
        out_specs=(wide, wide, wide, thin),
        check_vma=False,
    )
```

```python
import math

import jax
import jax.numpy as jnp
from jax import lax
from jax.experimental import pallas as pl
from jax.experimental.pallas import tpu as pltpu
from jax.sharding import Mesh, PartitionSpec as P

F32 = jnp.float32
BF16 = jnp.bfloat16
LOG2E = 1.4426950408889634
NEG = -1e30
GROUP = 8
HALF = 128
ROWS = 256
AUX = 16
PACK = ROWS + AUX
NEAR = (0, 1, -1, 2, -2, 3, -3, 4)
Z, Y, C = "z", ("y_hi", "y_lo"), "core"
COLUMN = ("y_hi", "y_lo", "core")
VMEM_LIMIT = 20 * 1024 * 1024
vmem = pl.BlockSpec(memory_space=pltpu.VMEM)
smem = pl.BlockSpec(memory_space=pltpu.SMEM)
hbm = pl.BlockSpec(memory_space=pl.ANY)


def call(kernel, outs, in_specs, scratch=(), flops=0, out_spec=None, limit=VMEM_LIMIT):
    return pl.pallas_call(
        kernel,
        out_shape=outs,
        in_specs=in_specs,
        out_specs=out_spec or jax.tree.map(lambda _: vmem, outs),
        scratch_shapes=list(scratch),
        compiler_params=pltpu.CompilerParams(vmem_limit_bytes=limit),
        cost_estimate=pl.CostEstimate(flops=flops, bytes_accessed=4 << 20, transcendentals=0),
    )


def dot(a, b, ca, cb):
    return lax.dot_general(a, b, (((ca,), (cb,)), ((), ())), preferred_element_type=F32)


def split_rows(row, first=0):
    high = row.astype(BF16).astype(F32)
    middle = (row - high).astype(BF16).astype(F32)
    low = row - high - middle
    at = lax.broadcasted_iota(jnp.int32, (AUX, row.shape[1]), 0) - first
    return jnp.where(at == 0, high, jnp.where(at == 1, middle, jnp.where(at == 2, low, 0.0)))


def join_rows(rows, first=0):
    rows = rows.astype(F32)
    return rows[first : first + 1] + rows[first + 1 : first + 2] + rows[first + 2 : first + 3]


def running_sum(row):
    lane = lax.broadcasted_iota(jnp.int32, row.shape, 1)
    step = 1
    while step < HALF:
        row = row + jnp.where(lane >= step, pltpu.roll(row, step, 1), 0.0)
        step *= 2
    return row


def place_of():
    z, y, core = lax.axis_index(Z), lax.axis_index("y_hi") * 2 + lax.axis_index("y_lo"), lax.axis_index(C)
    return z, y, core, y * 2 + core


def slot_low(span_ref, slot):
    return jnp.minimum(span_ref[2 * slot], span_ref[2 * slot + 1])


def own_swap(span_ref):
    z, _, _, column = place_of()
    slot = 2 * (z * GROUP + column)
    return (span_ref[slot] > span_ref[slot + 1]).astype(jnp.int32)


def near_z(z, e):
    return lax.rem(z + (NEAR[e] + GROUP), GROUP)


def near_column(y, core, at):
    offset, other = (0, 1, 3, 2)[at // 2], at % 2
    return lax.rem(y + offset, 4) * 2 + (1 - core if other else core)


def half_rows(half):
    return pl.ds(pl.multiple_of(HALF * half, HALF), HALF)


def table_lanes(table, z, own, low, high):
    sub = lax.broadcasted_iota(jnp.int32, (GROUP, HALF), 0)
    lane = lax.broadcasted_iota(jnp.int32, (GROUP, HALF), 1)
    table = jnp.where((sub == z) & (lane == 2 * own), low, table)
    return jnp.where((sub == z) & (lane == 2 * own + 1), high, table)


def pack_kernel(
    span_ref, q_ref, k_ref, v_ref, g_ref, f_ref, qg_ref, kv_ref, ids_ref, qg, kv, sems
):
    swap = own_swap(span_ref)
    copies = []
    for half in range(2):
        source = half_rows(jnp.bitwise_xor(half, swap))
        target = pl.ds(HALF * half, HALF)
        for ref, out, lanes in (
            (k_ref, kv, pl.ds(0, HALF)),
            (v_ref, kv, pl.ds(HALF, HALF)),
            (q_ref, qg, pl.ds(0, HALF)),
            (g_ref, qg, pl.ds(HALF, HALF)),
        ):
            copies.append((ref.at[source, :], out.at[target, lanes]))
    copies = [pltpu.make_async_copy(a, b, sems.at[i]) for i, (a, b) in enumerate(copies)]
    for copy in copies:
        copy.start()
    gates = [f_ref[0:1, 0:HALF], f_ref[0:1, HALF:ROWS]]
    gates = [jnp.where(swap == 1, gates[1 - half], gates[half]) for half in range(2)]
    gates = running_sum(jnp.concatenate(gates, 0))
    for half in range(2):
        rows = split_rows(gates[half : half + 1, :]).astype(BF16)
        qg[ROWS:PACK, HALF * half : HALF * (half + 1)] = rows
        kv[ROWS:PACK, HALF * half : HALF * (half + 1)] = rows
    ids = jnp.zeros((GROUP, HALF), jnp.int32)
    for z in range(GROUP):
        for b in range(GROUP):
            low = slot_low(span_ref, z * GROUP + b)
            ids = table_lanes(ids, z, b, low, 127 - low)
    ids_ref[...] = ids
    for copy in copies:
        copy.wait()
    run_copies([(kv, kv_ref), (qg, qg_ref)], sems)


def totals_kernel(*refs):
    blocks, out_ref, aux, sems = refs[:8], refs[8], refs[9], refs[10]
    z, _, _, own = place_of()
    copies = []
    for at, block in enumerate(blocks):
        last = block.shape[0] - AUX
        copies.append((block.at[pl.ds(last, AUX), :], aux.at[at]))
    run_copies(copies, sems)
    table = jnp.zeros((GROUP, HALF), F32)
    for e in range(GROUP):
        row = join_rows(aux[e])
        ends = [row[:, HALF * (half + 1) - 1 : HALF * (half + 1)] for half in range(2)]
        table = table_lanes(table, near_z(z, e), own, *ends)
    out_ref[...] = table


def totals_kernel(*refs):
    blocks, out_ref, aux, sems = refs[:8], refs[8], refs[9], refs[10]
    z, _, _, own = place_of()
    copies = []
    for at, block in enumerate(blocks):
        last = block.shape[0] - AUX
        copies.append((block.at[pl.ds(last, AUX), :], aux.at[at]))
    run_copies(copies, sems)
    table = jnp.zeros((GROUP, HALF), F32)
    for e in range(GROUP):
        row = join_rows(aux[e])
        ends = [row[:, HALF * (half + 1) - 1 : HALF * (half + 1)] for half in range(2)]
        table = table_lanes(table, near_z(z, e), own, *ends)
    out_ref[...] = table


def ids_kernel(span_ref, out_ref):
    table = jnp.zeros((GROUP, HALF), jnp.int32)
    for z in range(GROUP):
        for b in range(GROUP):
            low = slot_low(span_ref, z * GROUP + b)
            table = table_lanes(table, z, b, low, 127 - low)
    out_ref[...] = table


def run_copies(copies, sems):
    copies = [pltpu.make_async_copy(a, b, sems.at[i]) for i, (a, b) in enumerate(copies)]
    for copy in copies:
        copy.start()
    for copy in copies:
        copy.wait()


def whole_keys(key_refs, last):
    if len(key_refs) == 4:
        last[HALF:PACK, :] = key_refs[2][...]
        last[0:HALF, :] = key_refs[3][...]
        return [*key_refs[:2], last]
    return key_refs


def gate_columns(ks, e, columns):
    row = join_rows(ks[e][ROWS:PACK, :]) * LOG2E
    for half in range(2):
        part = row[:, HALF * half : HALF * (half + 1)]
        columns[half] = jnp.transpose(jnp.broadcast_to(part, (HALF, HALF)))


def ahead_of():
    return lax.broadcasted_iota(jnp.int32, (HALF, HALF), 0) - lax.broadcasted_iota(
        jnp.int32, (HALF, HALF), 1
    )


def lanes_of(d):
    return pl.ds(pl.multiple_of(HALF * d, HALF), HALF)


def place_queries(query_refs, y, core, qs, qt, gates):
    for at, ref in enumerate(query_refs):
        d = near_column(y, core, at)
        for half in range(2):
            block = ref[HALF * half : HALF * (half + 1), :]
            qs[half, lanes_of(d), :] = block
            qt[0, half, :, lanes_of(d)] = jnp.transpose(block[:, 0:HALF])
            qt[1, half, :, lanes_of(d)] = jnp.transpose(block[:, HALF:ROWS])
        gates[d] = ref[ROWS:PACK, :]


def stats_kernel(scale, first, span_ref, *refs):
    z, y, core, own = place_of()
    if first:
        qt, wq = refs[:2]
        rest, refs = refs[2:], ()
        count = 3
        key_refs, (one_ref, two_ref), (last, columns) = rest[:4], rest[4:6], rest[6:]
        ks = whole_keys(key_refs, last)
    else:
        count = 5
        query_refs, ks = refs[:8], refs[8:13]
        one_ref, two_ref, own_ref, qs, qt, wq, columns, gates = refs[13:]
        place_queries(query_refs, y, core, qs, qt, gates)
        for d in range(GROUP):
            row = join_rows(gates[d]) * LOG2E
            wq[0, d : d + 1, :] = row[:, 0:HALF]
            wq[1, d : d + 1, :] = row[:, HALF:ROWS]
    ahead = ahead_of()
    lows = [slot_low(span_ref, z * GROUP + d) for d in range(GROUP)]

    def tile_stats(scores, upstream):
        best = jnp.max(scores, axis=0, keepdims=True)
        factor = jnp.exp2(scores - best)
        return (
            best,
            jnp.sum(factor, axis=0, keepdims=True),
            jnp.sum(factor * upstream, axis=0, keepdims=True),
        )

    for e in range(count):
        gate_columns(ks, e, columns)
        key_span = slot_low(span_ref, near_z(z, first + e) * GROUP + own)
        key_low, value_low = ks[e][0:HALF, 0:HALF], ks[e][0:HALF, HALF:ROWS]
        column = columns[0]
        column2 = jnp.concatenate([column, column], 1)
        for pair in range(GROUP // 2):
            lanes = slice(ROWS * pair, ROWS * (pair + 1))
            w = jnp.concatenate([wq[1, 2 * pair + i : 2 * pair + i + 1, :] for i in range(2)], 1)
            scores = dot(key_low, qt[0, 1, :, lanes], 1, 0) * scale + (w - column2)
            upstream = dot(value_low, qt[1, 1, :, lanes], 1, 0)
            for at, row in enumerate(tile_stats(scores, upstream)):
                one_ref[e, at : at + 1, lanes] = row
        for d in range(GROUP):
            half = (key_span > lows[d]).astype(jnp.int32)
            rows, lanes = half_rows(half), slice(HALF * d, HALF * (d + 1))
            scores = dot(ks[e][rows, 0:HALF], qt[0, half, :, lanes], 1, 0) * scale + (
                wq[half, d : d + 1, :] - columns[half]
            )
            if first + e == 0:
                scores = jnp.where(ahead <= jnp.where(own == d, 0, HALF), scores, NEG)
            upstream = dot(ks[e][rows, HALF:ROWS], qt[1, half, :, lanes], 1, 0)
            for at, row in enumerate(tile_stats(scores, upstream)):
                two_ref[e, at : at + 1, lanes] = row
        if first + e == 0:
            w, lanes = wq[1, pl.ds(own, 1), :], lanes_of(own)
            scores = dot(ks[0][HALF:ROWS, 0:HALF], qt[0, 1, :, lanes], 1, 0) * scale
            scores = jnp.where(ahead <= 0, scores + (w - columns[1]), NEG)
            upstream = dot(ks[0][HALF:ROWS, HALF:ROWS], qt[1, 1, :, lanes], 1, 0)
            for at, row in enumerate(tile_stats(scores, upstream)):
                own_ref[at : at + 1, :] = row


def down(x):
    return jnp.sum(x, axis=0, keepdims=True)


def key_ranks(span_ref, z, own):
    sub = lax.broadcasted_iota(jnp.int32, (GROUP, HALF), 0)
    rank = jnp.zeros((GROUP, HALF), jnp.int32)
    for e in range(GROUP):
        rank = jnp.where(sub == e, slot_low(span_ref, near_z(z, e) * GROUP + own), rank)
    return rank


def tile_rows(near_ref, far_ref, at, lanes):
    return jnp.concatenate([near_ref[:, at, lanes], far_ref[:, at, lanes]], 0)


def merge_kernel(
    span_ref, ids_ref, t0, t1, t2, t3, near1, near2, own_ref, far1, far2, out_ref, place_ref
):
    z, y, core, own = place_of()
    ids, totals = ids_ref[...], t0[...] + t1[...] + t2[...] + t3[...]
    lows = [slot_low(span_ref, near_z(z, e) * GROUP + own) for e in range(GROUP)]
    lows += [slot_low(span_ref, z * GROUP + d) for d in range(GROUP)]
    places = {}
    for at in range(2 * GROUP):
        for half in range(2):
            span = 127 - lows[at] if half else lows[at]
            before = jnp.where(ids < span, totals, 0.0)
            place = jnp.sum(down(before), axis=1, keepdims=True) * LOG2E
            row = 2 * GROUP * (at // GROUP) + GROUP * half + at % GROUP
            places[row] = jnp.broadcast_to(place, (1, HALF))
            place_ref[row : row + 1, :] = places[row]
    key_low = jnp.concatenate([places[i] for i in range(0, 8)], 0)
    key_high = jnp.concatenate([places[i] for i in range(8, 16)], 0)
    ranks = key_ranks(span_ref, z, own)

    def finish(best, total, weighted, at, d):
        some = total > 0.0
        safe = jnp.where(some, total, 1.0)
        lse = jnp.where(some, best + jnp.log2(safe), NEG)
        delta = jnp.where(some, weighted / safe, 0.0)
        for copy in range(GROUP):
            out_ref[copy, at + d : at + d + 1, :] = lse
            out_ref[copy, at + 8 + d : at + 9 + d, :] = delta

    for d in range(GROUP):
        lanes = slice(HALF * d, HALF * (d + 1))
        one = [tile_rows(near1, far1, at, lanes) for at in range(3)]
        two = [tile_rows(near2, far2, at, lanes) for at in range(3)]
        high = ranks > lows[GROUP + d]
        query_low, query_high = places[16 + d], places[24 + d]
        first = one[0] + (query_high - key_low)
        second = two[0] + jnp.where(high, query_high - key_high, query_low - key_low)
        mine = own == d
        third = jnp.where(mine, own_ref[0:1, :], NEG)
        best = jnp.maximum(
            jnp.max(jnp.maximum(first, jnp.where(high, second, NEG)), axis=0, keepdims=True), third
        )
        first_weight = jnp.exp2(first - best)
        second_weight = jnp.where(high, jnp.exp2(second - best), 0.0)
        third_weight = jnp.where(mine, jnp.exp2(third - best), 0.0)
        sums = [
            down(one[at] * first_weight + two[at] * second_weight)
            + own_ref[at : at + 1, :] * third_weight
            for at in (1, 2)
        ]
        finish(best, sums[0], sums[1], 0, d)
        low = jnp.where(high, NEG, second)
        best = jnp.max(low, axis=0, keepdims=True)
        weight = jnp.where(high, 0.0, jnp.exp2(low - best))
        sums = [down(two[at] * weight) for at in (1, 2)]
        finish(best, sums[0], sums[1], 16, d)


def combine_kernel(
    span_ref, stats_ref, place_ref, wq_ref, near1, near2, own_ref, far1, far2, gate_ref, delta_ref, out_ref
):
    z, y, core, own = place_of()
    lses, deltas = [None, None], [None, None]
    for half, at in ((1, 0), (0, 16)):
        lse = [stats_ref[b, at : at + 8, :] for b in range(GROUP)]
        best = lse[0]
        for b in range(1, GROUP):
            best = jnp.maximum(best, lse[b])
        total = jnp.zeros((GROUP, HALF), F32)
        weighted = jnp.zeros((GROUP, HALF), F32)
        for b in range(GROUP):
            weight = jnp.exp2(lse[b] - best)
            total = total + weight
            weighted = weighted + weight * stats_ref[b, at + 8 : at + 16, :]
        lses[half] = best + jnp.log2(total)
        deltas[half] = weighted / total
        gate_ref[half] = wq_ref[half] - lses[half]
        delta_ref[half] = deltas[half]
    key_low, key_high = place_ref[0:8, :], place_ref[8:16, :]
    ranks = key_ranks(span_ref, z, own)
    sub = lax.broadcasted_iota(jnp.int32, (GROUP, HALF), 0)
    low_sum = jnp.zeros((GROUP, HALF), F32)
    high_sum = jnp.zeros((GROUP, HALF), F32)
    for d in range(GROUP):
        lanes = slice(HALF * d, HALF * (d + 1))
        one = [tile_rows(near1, far1, at, lanes) for at in range(3)]
        two = [tile_rows(near2, far2, at, lanes) for at in range(3)]
        high = ranks > slot_low(span_ref, z * GROUP + d)
        lse_low, lse_high = lses[0][d : d + 1, :], lses[1][d : d + 1, :]
        delta_low, delta_high = deltas[0][d : d + 1, :], deltas[1][d : d + 1, :]
        query_low, query_high = place_ref[16 + d : 17 + d, :], place_ref[24 + d : 25 + d, :]
        first = jnp.exp2(one[0] + (query_high - key_low) - lse_high)
        first = first * (one[2] - delta_high * one[1])
        shift = jnp.where(high, query_high - key_high - lse_high, query_low - key_low - lse_low)
        second = jnp.exp2(two[0] + shift)
        second = second * (two[2] - jnp.where(high, delta_high, delta_low) * two[1])
        third = jnp.exp2(own_ref[0:1, :] - lse_high)
        third = third * (own_ref[2:3, :] - delta_high * own_ref[1:2, :])
        low_sum = low_sum + first + jnp.where(high, 0.0, second)
        high_sum = high_sum + jnp.where(high, second, 0.0)
        high_sum = high_sum + jnp.where((sub == 0) & (own == d), third, 0.0)
    low_sum = -jnp.sum(low_sum, axis=1, keepdims=True)
    high_sum = -jnp.sum(high_sum, axis=1, keepdims=True)
    table = jnp.zeros((GROUP, HALF), F32)
    for e in range(GROUP):
        row = slice(e, e + 1)
        table = table_lanes(table, near_z(z, e), own, low_sum[row, :], high_sum[row, :])
    for copy in range(GROUP):
        out_ref[copy] = table


def beyond_kernel(span_ref, ids_ref, tables_ref, a_ref, b_ref, c_ref, out_ref, a_out, b_out, c_out):
    z, y, core, own = place_of()
    table = tables_ref[0]
    for b in range(1, GROUP):
        table = table + tables_ref[b]
    ids = ids_ref[...]
    lane = lax.broadcasted_iota(jnp.int32, (1, ROWS), 1)
    rows = []
    for e in range(GROUP):
        low = slot_low(span_ref, near_z(z, e) * GROUP + own)
        row = jnp.zeros((1, ROWS), F32)
        for half, span in ((0, low), (1, 127 - low)):
            value = jnp.sum(down(jnp.where(ids > span, table, 0.0)), axis=1, keepdims=True)
            row = jnp.where(lane == HALF * (half + 1) - 1, value, row)
        rows.append(row)
        out_ref[e : e + 1, :] = row
    for row, source, target in zip(rows[5:], (a_ref, b_ref, c_ref), (a_out, b_out, c_out)):
        last = source.shape[0] - AUX
        target[0:last, :] = source[0:last, :]
        aux = join_rows(source[last : last + AUX, :]) + row
        target[last : last + AUX, :] = split_rows(aux).astype(BF16)


def grads_kernel(scale, first, count, pieces, span_ref, qs, qt, gate_ref, delta_ref, place_ref, *refs):
    z, y, core, own = place_of()
    key_refs, refs = refs[:pieces], refs[pieces:]
    if first == 5:
        dqt_out, refs = refs[0], refs[1:]
        outs, scratch = refs[:4], refs[4:]
        dqt, scratch = scratch[0], scratch[1:]
        dqt[...] = jnp.zeros_like(dqt)
    elif first == 0:
        before, beyond, dqt_out, refs = refs[0], refs[1], refs[2], refs[3:]
        outs, scratch = refs[:3], refs[3:]
        dqt, scratch = scratch[0], scratch[1:]
        dqt[...] = before[...].astype(F32)
    else:
        before, beyond, up3, down3, up4, down4, dq_ref = refs[:7]
        outs, scratch = refs[7:9], refs[9:]
        dqt, scratch = scratch[0], scratch[1:]
        dqt[...] = before[...].astype(F32)
    last, columns, pg = scratch
    ks = whole_keys(key_refs, last)
    ahead = ahead_of()
    inverse = 1.0 / math.sqrt(HALF)
    lows = [slot_low(span_ref, z * GROUP + d) for d in range(GROUP)]

    def query_gate(half, d, key_place):
        place = place_ref[pl.ds(16 + 8 * half + d, 1), :]
        return gate_ref[half, d : d + 1, :] + (place - key_place)

    for e in range(count):
        number = first + e
        gate_columns(ks, e, columns)
        key_span = slot_low(span_ref, near_z(z, number) * GROUP + own)
        key_low, value_low = ks[e][0:HALF, 0:HALF], ks[e][0:HALF, HALF:ROWS]
        turned = jnp.transpose(ks[e][0:ROWS, 0:HALF])
        column = columns[0]
        column2 = jnp.concatenate([column, column], 1)
        place = place_ref[number : number + 1, :]
        probs1, grads1, probs2, grads2 = [], [], ([], []), ([], [])
        total = jnp.zeros((HALF, HALF), F32)
        for pair in range(GROUP // 2):
            both, lanes = (2 * pair, 2 * pair + 1), slice(ROWS * pair, ROWS * (pair + 1))
            w = jnp.concatenate([query_gate(1, d, place) for d in both], 1)
            shift = jnp.concatenate([delta_ref[1, d : d + 1, :] for d in both], 1)
            probs = jnp.exp2(dot(key_low, qt[0, 1, :, lanes], 1, 0) * scale + (w - column2))
            grads = probs * (dot(value_low, qt[1, 1, :, lanes], 1, 0) - shift)
            probs1.append(probs.astype(BF16))
            grads1.append(grads.astype(BF16))
            total = total + grads[:, 0:HALF] + grads[:, HALF:ROWS]
        pg[0] = total
        pg[1] = jnp.zeros((HALF, HALF), F32)
        chosen = []
        for d in range(GROUP):
            half = (key_span > lows[d]).astype(jnp.int32)
            rows, lanes = half_rows(half), slice(HALF * d, HALF * (d + 1))
            chosen.append(qs[half, lanes, :])
            w = query_gate(half, d, place_ref[pl.ds(8 * half + number, 1), :])
            scores = dot(ks[e][rows, 0:HALF], qt[0, half, :, lanes], 1, 0) * scale
            probs = jnp.exp2(scores + (w - columns[half]))
            if number == 0:
                probs = jnp.where(ahead <= jnp.where(own == d, 0, HALF), probs, 0.0)
            upstream = dot(ks[e][rows, HALF:ROWS], qt[1, half, :, lanes], 1, 0)
            grads = probs * (upstream - delta_ref[half, d : d + 1, :])
            pg[half] += grads
            probs, grads = probs.astype(BF16), grads.astype(BF16)
            zero = jnp.zeros_like(probs)
            for side in range(2):
                probs2[side].append(jnp.where(half == side, probs, zero))
                grads2[side].append(jnp.where(half == side, grads, zero))
        chosen = jnp.concatenate(chosen, 0)
        side_probs, side_grads = (
            [jnp.concatenate(part, 1) for part in parts] for parts in (probs2, grads2)
        )
        value_parts = dot(jnp.concatenate(side_probs, 0), chosen[:, HALF:ROWS], 1, 0)
        key_parts = dot(jnp.concatenate(side_grads, 0), chosen[:, 0:HALF], 1, 0)
        dv = [
            value_parts[0:HALF, :] + dot(jnp.concatenate(probs1, 1), qs[1, :, HALF:ROWS], 1, 0),
            value_parts[HALF:ROWS, :],
        ]
        dk = [
            key_parts[0:HALF, :] + dot(jnp.concatenate(grads1, 1), qs[1, :, 0:HALF], 1, 0),
            key_parts[HALF:ROWS, :],
        ]
        for pair in range(GROUP // 2):
            lanes = slice(ROWS * pair, ROWS * (pair + 1))
            stack = jnp.concatenate([grads1[pair], side_grads[1][:, lanes]], 0)
            dqt[1, :, lanes] += dot(turned, stack, 1, 0)
            dqt[0, :, lanes] += dot(turned[:, 0:HALF], side_grads[0][:, lanes], 1, 0)
        if number == 0:
            lanes = lanes_of(own)
            scores = dot(ks[e][HALF:ROWS, 0:HALF], qt[0, 1, :, lanes], 1, 0) * scale
            probs = jnp.exp2(scores + (gate_ref[1, pl.ds(own, 1), :] - columns[1]))
            probs = jnp.where(ahead <= 0, probs, 0.0)
            upstream = dot(ks[e][HALF:ROWS, HALF:ROWS], qt[1, 1, :, lanes], 1, 0)
            grads = probs * (upstream - delta_ref[1, pl.ds(own, 1), :])
            low_grads, block = grads.astype(BF16), qs[1, lanes_of(own), :]
            dv[1] = dv[1] + dot(probs.astype(BF16), block[:, HALF:ROWS], 1, 0)
            dk[1] = dk[1] + dot(low_grads, block[:, 0:HALF], 1, 0)
            dqt[1, :, lanes] += dot(turned[:, HALF:ROWS], low_grads, 1, 0)
            pg[1] += grads

        for half in range(2):
            rows = slice(HALF * half, HALF * (half + 1))
            key_part, value_part = dk[half] * inverse, dv[half]
            row = -down(jnp.transpose(pg[half]))
            if number < 5:
                row = row + beyond[number : number + 1, rows]
            out, base, keep_aux = outs[e], HALF * half, True
            if number == 7:
                out, base, keep_aux = outs[2 + half], 0, half == 1
            if number in (3, 4):
                arrived = (up3, down3)[number - 3]
                key_part = key_part + arrived[rows, 0:HALF].astype(F32)
                value_part = value_part + arrived[rows, HALF:ROWS].astype(F32)
                row = row + join_rows(arrived[ROWS:PACK, rows])
                if number == 3:
                    row = row + join_rows(up4[HALF : HALF + AUX, rows])
                if half == 4 - number:
                    arrived = (up4, down4)[number - 3]
                    key_part = key_part + arrived[0:HALF, 0:HALF].astype(F32)
                    value_part = value_part + arrived[0:HALF, HALF:ROWS].astype(F32)
            out[base : base + HALF, 0:HALF] = key_part.astype(BF16)
            out[base : base + HALF, HALF:ROWS] = value_part.astype(BF16)
            aux_out = outs[3] if number == 7 else out
            aux_base = HALF if number == 7 else ROWS
            aux_out[aux_base : aux_base + AUX, rows] = split_rows(row).astype(BF16)

    if first != 3:
        dqt_out[...] = dqt[...].astype(BF16)
    else:
        for d in range(GROUP):
            for half in range(2):
                part = jnp.transpose(dqt[half, :, HALF * d : HALF * (d + 1)]) * inverse
                dq_ref[d, HALF * half : HALF * (half + 1), :] = part.astype(BF16)


def final_kernel(
    span_ref, dq_parts, p0, p1, p2, p3, p4, dq_ref, dk_ref, dv_ref, f_ref
):
    z, y, core, own = place_of()
    swap = own_swap(span_ref)
    parts = (p0, p1, p2, p3, p4)
    halves = []
    for half in range(2):
        rows = slice(HALF * half, HALF * (half + 1))
        target = half_rows(jnp.bitwise_xor(half, swap))
        total = dq_parts[0, rows, :].astype(F32)
        for b in range(1, GROUP):
            total = total + dq_parts[b, rows, :].astype(F32)
        dq_ref[target, :] = total.astype(BF16)
        total = p0[rows, :].astype(F32)
        for part in parts[1:]:
            total = total + part[rows, :].astype(F32)
        total = total.astype(BF16)
        dk_ref[target, :] = total[:, 0:HALF]
        dv_ref[target, :] = total[:, HALF:ROWS]
        row = join_rows(p0[ROWS:PACK, rows])
        for part in parts[1:]:
            row = row + join_rows(part[ROWS:PACK, rows])
        halves.append(row)
    both = jnp.concatenate(halves, 0)
    both = jnp.sum(both, axis=1, keepdims=True) - running_sum(both) + both
    for half in range(2):
        lanes = slice(HALF * half, HALF * (half + 1))
        f_ref[:, lanes] = jnp.where(swap == 1, both[1 - half : 2 - half, :], both[half : half + 1, :])


def fetch(x, axis, size, offset):
    return lax.ppermute(x, axis, [((i + offset) % size, i) for i in range(size)])


def local(queries, key_vectors, value_vectors, out_grad, log_forget, span_order):
    scale = LOG2E / math.sqrt(HALF)

    def struct(shape, kind):
        return jax.ShapeDtypeStruct(shape, kind)

    block = struct((PACK, ROWS), BF16)
    table = struct((GROUP, HALF), F32)
    qg, kv, ids = call(
        pack_kernel,
        (block, block, struct((GROUP, HALF), jnp.int32)),
        [smem] + [hbm] * 4 + [vmem],
        [pltpu.VMEM((PACK, ROWS), BF16)] * 2 + [pltpu.SemaphoreType.DMA((8,))],
        out_spec=(hbm, hbm, vmem),
        limit=62 * 1024 * 1024,
    )(span_order, queries[0], key_vectors[0], value_vectors[0], out_grad[0], log_forget)
    up1, down1, up2, down2 = [fetch(kv, Z, 8, o) for o in (1, -1, 2, -2)]
    mine = [qg] + [fetch(qg, Y, 4, o) for o in (1, -1, 2)]
    up3, down3 = fetch(up2, Z, 8, 1), fetch(down2, Z, 8, -1)
    theirs = [fetch(x, C, 2, 1) for x in mine]
    far_low = fetch(down2[:HALF], Z, 8, -2)
    far_high = fetch(up2[HALF:], Z, 8, 2)
    query_blocks = [x for pair in zip(mine, theirs) for x in pair]
    near_keys = [kv, up1, down1, up2, down2]
    far_keys = [up3, down3, far_high, far_low]

    totals = call(
        totals_kernel,
        table,
        [hbm] * 8,
        [pltpu.VMEM((8, AUX, ROWS), BF16), pltpu.SemaphoreType.DMA((8,))],
    )(*near_keys, *far_keys[:3])
    totals = totals + fetch(totals, C, 2, 1)
    totals = [totals] + [fetch(totals, Y, 4, o) for o in (1, -1, 2)]

    def tiles(count):
        return struct((count, 3, GROUP * HALF), F32)

    gates = struct((2, GROUP, HALF), F32)
    near1, near2, own, qs, qt, wq = call(
        lambda *refs: stats_kernel(scale, 0, *refs),
        (
            tiles(5),
            tiles(5),
            struct((GROUP, HALF), F32),
            struct((2, GROUP * HALF, ROWS), BF16),
            struct((2, 2, HALF, GROUP * HALF), BF16),
            gates,
        ),
        [smem] + [vmem] * 13,
        [pltpu.VMEM((2, HALF, HALF), F32), pltpu.VMEM((GROUP, AUX, ROWS), BF16)],
        flops=1 << 31,
    )(span_order, *query_blocks, *near_keys)
    far1, far2 = call(
        lambda *refs: stats_kernel(scale, 5, *refs),
        (tiles(3), tiles(3)),
        [smem] + [vmem] * 6,
        [pltpu.VMEM((PACK, ROWS), BF16), pltpu.VMEM((2, HALF, HALF), F32)],
        flops=1 << 31,
    )(span_order, qt, wq, *far_keys)
    stats, place = call(
        merge_kernel,
        (struct((GROUP, 32, HALF), F32), struct((32, HALF), F32)),
        [smem] + [vmem] * 10,
    )(span_order, ids, *totals, near1, near2, own, far1, far2)
    stats = lax.all_to_all(stats, COLUMN, 0, 0, tiled=True)
    gate, delta, span_grads = call(
        combine_kernel,
        (gates, gates, struct((GROUP, GROUP, HALF), F32)),
        [smem] + [vmem] * 8,
    )(span_order, stats, place, wq, near1, near2, own, far1, far2)
    span_grads = lax.all_to_all(span_grads, COLUMN, 0, 0, tiled=True)
    square = pltpu.VMEM((2, HALF, HALF), F32)
    sum_t = struct((2, HALF, GROUP * HALF), BF16)

    def grads(first, count, keys, more, outs):
        return call(
            lambda *refs: grads_kernel(scale, first, count, len(keys), *refs),
            outs,
            [smem] + [vmem] * (5 + len(keys) + len(more)),
            [
                pltpu.VMEM((2, HALF, GROUP * HALF), F32),
                pltpu.VMEM((PACK, ROWS), BF16),
                square,
                square,
            ],
            flops=1 << 31,
        )(span_order, qs, qt, gate, delta, place, *keys, *more)

    low_piece, high_piece = struct((HALF, ROWS), BF16), struct((HALF + AUX, ROWS), BF16)
    dqt, part3, part3d, part4, part4d_high = grads(
        5, 3, far_keys, [], (sum_t, block, block, low_piece, high_piece)
    )
    beyond, part3, part3d, part4d_high = call(
        beyond_kernel,
        (struct((GROUP, ROWS), F32), block, block, high_piece),
        [smem] + [vmem] * 5,
    )(span_order, ids, span_grads, part3, part3d, part4d_high)
    arrived_up3, arrived_down3 = fetch(part3, Z, 8, -1), fetch(part3d, Z, 8, 1)
    arrived_up4, arrived_down4 = fetch(part4d_high, Z, 8, -2), fetch(part4, Z, 8, 2)
    dqt, part0, part1, part1d = grads(0, 3, near_keys[:3], [dqt, beyond], (sum_t, block, block, block))
    arrived1, arrived1d = fetch(part1, Z, 8, -1), fetch(part1d, Z, 8, 1)
    dq_parts, part2, part2d = grads(
        3,
        2,
        near_keys[3:],
        [dqt, beyond, arrived_up3, arrived_down3, arrived_up4, arrived_down4],
        (struct((GROUP, ROWS, HALF), BF16), block, block),
    )
    arrived2, arrived2d = fetch(part2, Z, 8, -2), fetch(part2d, Z, 8, 2)
    dq_parts = lax.all_to_all(dq_parts, COLUMN, 0, 0, tiled=True)
    rows = struct((ROWS, HALF), BF16)
    dq, dk, dv, forget = call(
        final_kernel, (rows, rows, rows, struct((1, ROWS), F32)), [smem] + [vmem] * 6
    )(span_order, dq_parts, part0, arrived1, arrived1d, arrived2, arrived2d)
    return dq[None], dk[None], dv[None], forget


def solution(mesh):
    fine = Mesh(mesh.devices.reshape(8, 2, 2, 2, 4), ("z", "y_hi", "y_lo", "core", "head"))
    rows = ("z", "y_hi", "y_lo", "core")
    wide, thin = P("head", rows, None), P("head", rows)
    return jax.shard_map(
        local,
        mesh=fine,
        in_specs=(wide, wide, wide, wide, thin, P()),
        out_specs=(wide, wide, wide, thin),
        check_vma=False,
    )
```
